256 devices in a mesh: rep: 8 (over y, core), shard: 32 (over x, z).
Axes of the slice: x: 4, y: 4, z: 8, core: 2. Of those that a mesh axis runs over, the one named last changes fastest.
Arguments:
- grad_out: bfloat16 [8, 4096, 8192], P('rep', 'shard'), may hold values from -6 to 6
- error_out: bfloat16 [8, 4096, 8192], P('rep', 'shard'), may hold values from -4 to 4
- basis_out: float32 [8192, 32], replicated, may hold values from -0.0625 to 0.0625
- overflow: int32 [8], P('rep'), may hold values from 0 to 1, as said below
Outputs:
- update_out: bfloat16 [4096, 8192], P('shard')
- new_error_out: bfloat16 [8, 4096, 8192], P('rep', 'shard')
- new_basis_out: float32 [8192, 32], replicated
The draws below stay inside these ranges and needn't reach their ends.
Inputs may be any that keep to these rules, and one draw needn't show every extreme that they name: `overflow`: at least one replica's flag is 1, at least one is 0, and at most half of the 8 replicas have flag 1.
All inputs are finite; a program needn't handle non-finite values.
Results may differ from the reference program's by a relative error of at most 0.002.
Values sent between devices are 32-bit elements; how exact they have to be, the bound alone decides.
A program may use at most 64 MiB of HBM per device.

```python
import jax
import jax.numpy as jnp
from jax import lax

D = 8192
RANK = 32
ROWS = 4096
N_REP = 8


def draw_overflow(key, part):
    key = jax.random.fold_in(key, 5)
    count_key, order_key = jax.random.split(key)
    skipped = jax.random.randint(count_key, (), 1, N_REP // 2 + 1, dtype=jnp.int32)
    ranking = jax.random.permutation(order_key, N_REP).astype(jnp.int32)
    return (ranking < skipped).astype(jnp.int32)


def block_levels(own_key, extent, cuts, smallest, largest):
    def one(position, blocks):
        heights = jax.random.uniform(jax.random.fold_in(jax.random.fold_in(own_key, 6), position), (blocks,), jnp.float32, smallest / len(cuts), largest / len(cuts))
        return jnp.repeat(jnp.exp(heights), extent[position] // blocks).reshape((-1,) + (1,) * (len(extent) - position - 1))

    loudness = one(*cuts[0])
    for cut in cuts[1:]:
        loudness = loudness * one(*cut)
    return loudness


def scatter_about(stream_key, shape, deviation, most, shards=(), kind=jnp.bfloat16):
    loudness = block_levels(stream_key, shape, shards, -0.22, 0.18) if shards else 1.0
    values = jax.random.normal(stream_key, shape, jnp.float32) * deviation * loudness
    return jnp.minimum(jnp.maximum(values, -most), most).astype(kind)


def setup_inputs(seed: int = 0) -> dict:
    keys = jax.random.split(jax.random.key(seed), 5)
    grad_out = scatter_about(keys[0], (N_REP, ROWS, D), 1.0, 6.0, ((0, 8), (1, 32)))
    error_out = scatter_about(keys[1], (N_REP, ROWS, D), 0.5, 4.0, ((0, 8), (1, 32)))
    basis_out = scatter_about(keys[2], (D, RANK), D ** -0.5, 0.0625, (), jnp.float32)
    overflow = draw_overflow(jax.random.fold_in(keys[4], 71), 0)
    return dict(grad_out=grad_out, error_out=error_out, basis_out=basis_out, overflow=overflow)


def reference(grad_out, error_out, basis_out, overflow):
    healthy = (1 - overflow).astype(jnp.float32)
    kept_total = jnp.sum(healthy)
    corrected = grad_out.astype(jnp.float32) + error_out.astype(jnp.float32)
    projected = jnp.einsum('rkc,cj->rkj', corrected, basis_out, precision=lax.Precision.HIGHEST)
    left = jnp.einsum('r,rkj->kj', healthy, projected, precision=lax.Precision.HIGHEST) / kept_total
    gram = jnp.dot(left.T, left, precision=lax.Precision.HIGHEST)
    shifted = gram + 1e-05 * (jnp.trace(gram) / RANK) * jnp.eye(RANK, dtype=jnp.float32)
    lower = jnp.linalg.cholesky(shifted)
    ortho = jax.scipy.linalg.solve_triangular(lower, left.T, lower=True).T
    columns = jnp.einsum('rkc,kj->rcj', corrected, ortho, precision=lax.Precision.HIGHEST)
    new_basis_out = jnp.einsum('r,rcj->cj', healthy, columns, precision=lax.Precision.HIGHEST) / kept_total
    approx = jnp.dot(ortho, new_basis_out.T, precision=lax.Precision.HIGHEST)
    update_out = approx.astype(jnp.bfloat16)
    new_error_out = jnp.where(healthy[:, None, None] > 0.5, corrected - approx[None], error_out.astype(jnp.float32)).astype(jnp.bfloat16)
    return (update_out, new_error_out, new_basis_out)
```

```python
import functools

import jax
import jax.numpy as jnp
from jax import lax
from jax.experimental import pallas as pl
from jax.experimental.pallas import tpu as pltpu
from jax.sharding import PartitionSpec as P

MESH = pl.DeviceIdType.MESH
F32, BF16 = jnp.float32, jnp.bfloat16
D, RANK, ROWS = 8192, 32, 128
CHUNKS = 4
CHUNK = D // CHUNKS
NY, NX, NZ = 4, 4, 8


def pieces(value):
    first = value.astype(BF16)
    rest = value - first.astype(F32)
    second = rest.astype(BF16)
    third = (rest - second.astype(F32)).astype(BF16)
    return first, second, third


def full_dot(a, b, dims):
    return lax.dot_general(a, b, (dims, ((), ())), precision=lax.Precision.HIGHEST, preferred_element_type=F32)


def inverse_factor(gram):
    row = lax.broadcasted_iota(jnp.int32, (RANK, 128), 0)
    lane = lax.broadcasted_iota(jnp.int32, (RANK, 128), 1)
    diagonal = row == lane
    trace = jnp.sum(jnp.where(diagonal, gram, 0.0), axis=(0, 1), keepdims=True)
    shift = 1e-05 * (trace / RANK)
    work = jnp.where(lane < RANK, gram, 0.0) + jnp.where(diagonal, shift, 0.0)
    work = work + jnp.where(lane - RANK == row, 1.0, 0.0)
    for j in range(RANK - 1):
        column = jnp.broadcast_to(work[:, j : j + 1], (RANK, 128))
        scaled = work[j : j + 1, :] / column[j : j + 1, :]
        work = work - jnp.where(row > j, column, 0.0) * scaled
    pivots = jnp.sum(jnp.where(diagonal, work, 0.0), axis=1, keepdims=True)
    inverse = work * lax.rsqrt(pivots)
    return pltpu.roll(inverse, 128 - RANK, 1)


def reduce_kernel(
    grad_hbm, error_hbm, basis_hbm, overflow, nb_out, ortho_out,
    ge, bt, lc, ly, gx, gz, sp, rc, t1, r1, t2, r2, zb, nb, ov,
    in_sem, lc_s, lc_r, ly_s, ly_r, gx_s, gx_r, gz_s, gz_r, rc_s, rc_r,
    p1_s, p1_r, p2_s, p2_r, z_s, z_r, a2_s, a2_r, a1_s, a1_r, ac_s, ac_r, out_sem,
):
    rep, shard = lax.axis_index("rep"), lax.axis_index("shard")
    y, c = rep // 2, rep % 2
    x, z = shard // NZ, shard % NZ

    def at(y_, c_, x_, z_):
        return (y_ * 2 + c_, x_ * NZ + z_)

    partner = at(y, 1 - c, x, z)

    def along_y(d):
        return at((y + d) % NY, c, x, z)

    def along_x(d):
        return at(y, c, (x + d) % NX, z)

    def along_z(d):
        return at(y, c, x, (z + d) % NZ)

    def remote(src, dst, send, recv, device):
        return pltpu.make_async_remote_copy(
            src_ref=src, dst_ref=dst, send_sem=send, recv_sem=recv, device_id=device, device_id_type=MESH
        )

    sent = []

    def send(src, dst, send_sem, recv_sem, device):
        copy = remote(src, dst, send_sem, recv_sem, device)
        copy.start()
        sent.append(copy)

    def arrived(dst, recv_sem):
        remote(dst, dst, lc_s.at[0], recv_sem, partner).wait_recv()

    loads = []
    for k in range(CHUNKS):
        cols = pl.ds(k * CHUNK, CHUNK)
        group = [
            pltpu.make_async_copy(basis_hbm.at[:, cols], bt.at[:, cols], in_sem.at[0, k]),
            pltpu.make_async_copy(grad_hbm.at[:, cols], ge.at[pl.ds(0, ROWS), cols], in_sem.at[1, k]),
            pltpu.make_async_copy(error_hbm.at[:, cols], ge.at[pl.ds(ROWS, ROWS), cols], in_sem.at[2, k]),
        ]
        for copy in group:
            copy.start()
        loads.append(group)

    barrier = pltpu.get_barrier_semaphore()
    others = [partner]
    others += [along_y(d) for d in range(1, NY)] + [along_x(d) for d in range(1, NX)]
    others += [along_z(d) for d in range(1, NZ)]
    for other in others:
        pl.semaphore_signal(barrier, inc=1, device_id=other, device_id_type=MESH)

    health = jnp.full((8, 128), 1.0 - overflow[0].astype(F32), F32)
    acc = jnp.zeros((3 * RANK, 2 * ROWS), F32)
    for k in range(CHUNKS):
        for copy in loads[k]:
            copy.wait()
        cols = pl.ds(k * CHUNK, CHUNK)
        basis = jnp.concatenate(pieces(bt[:, cols]), axis=0)
        acc += lax.dot_general(basis, ge[:, cols], (((1,), (1,)), ((), ())), preferred_element_type=F32)
    both = acc[:RANK] + acc[RANK : 2 * RANK] + acc[2 * RANK :]
    lc[0, :RANK] = (both[:, :ROWS] + both[:, ROWS:]) * health[:1]
    lc[0, RANK:] = health

    pl.semaphore_wait(barrier, len(others))

    send(lc.at[0], lc.at[1], lc_s.at[0], lc_r.at[0], partner)
    arrived(lc.at[1], lc_r.at[0])
    ly[y] = lc[0] + lc[1]
    for d in range(1, NY):
        send(ly.at[y], ly.at[y], ly_s.at[d], ly_r.at[y], along_y(d))
    for d in range(1, NY):
        source = (y + d) % NY
        arrived(ly.at[source], ly_r.at[source])
    total = ly[0] + ly[1] + ly[2] + ly[3]
    kept = total[RANK : RANK + 1]
    left = total[:RANK] / kept

    gram = full_dot(left, jnp.concatenate([left] * 4, axis=0), ((1,), (1,)))
    lane_group = lax.broadcasted_iota(jnp.int32, (8, 128), 1) // RANK
    packed = gram[:8]
    for b in range(1, 4):
        packed = jnp.where(lane_group == b, gram[8 * b : 8 * b + 8], packed)
    gx[x] = packed
    for d in range(1, NX):
        send(gx.at[x], gx.at[x], gx_s.at[d], gx_r.at[x], along_x(d))

    weighted = jnp.concatenate(pieces(left * (health[:1] / kept)), axis=0)
    weighted = jnp.concatenate([weighted, weighted], axis=1)

    def product(block):
        cols = pl.ds(pl.multiple_of(block * 128, 512), 512)
        out = lax.dot_general(weighted, ge[:, cols], (((1,), (0,)), ((), ())), preferred_element_type=F32)
        return out[:RANK] + out[RANK : 2 * RANK] + out[2 * RANK :]

    first = (x, y)
    second = (y, x)
    along_first = (along_x, along_y)
    along_second = (along_y, along_x)
    order = [(d, h) for d in (1, 2, 3, 0) for h in range(2)]
    for i, (d, h) in enumerate(order):
        group = h * 16 + ((first[h] + d) % 4) * 4
        theirs = (1 - c) * 32 + group
        value = product(theirs)
        for q in range(4):
            sp[group + q] = value[:, q * 128 : (q + 1) * 128]
        send(sp.at[pl.ds(group, 4)], rc.at[pl.ds(group, 4)], rc_s.at[i], rc_r.at[i], partner)
    for i, (d, h) in enumerate(order):
        p = (first[h] + d) % 4
        group = h * 16 + p * 4
        value = product(c * 32 + group)
        arrived(rc.at[pl.ds(group, 4)], rc_r.at[i])
        if d == 0:
            for q in range(4):
                r1[h, p, q] = value[:, q * 128 : (q + 1) * 128] + rc[group + q]
        else:
            for q in range(4):
                t1[group + q] = value[:, q * 128 : (q + 1) * 128] + rc[group + q]
            send(t1.at[pl.ds(group, 4)], r1.at[h, first[h]], p1_s.at[h, d], p1_r.at[h, first[h]], along_first[h](d))

    for d in range(1, NX):
        source = (x + d) % NX
        arrived(gx.at[source], gx_r.at[source])
    gz[z] = gx[0] + gx[1] + gx[2] + gx[3]
    for d in range(1, NZ):
        send(gz.at[z], gz.at[z], gz_s.at[d], gz_r.at[z], along_z(d))

    for h in range(2):
        for d in range(1, 4):
            source = (first[h] + d) % 4
            arrived(r1.at[h, source], p1_r.at[h, source])
        for q in range(4):
            t2[h, q] = r1[h, 0, q] + r1[h, 1, q] + r1[h, 2, q] + r1[h, 3, q]
        for d in range(1, 4):
            q = (second[h] + d) % 4
            send(t2.at[h, q], r2.at[h, second[h]], p2_s.at[h, d], p2_r.at[h, second[h]], along_second[h](d))
        r2[h, second[h]] = t2[h, second[h]]
    for h in range(2):
        for d in range(1, 4):
            source = (second[h] + d) % 4
            arrived(r2.at[h, source], p2_r.at[h, source])
        zb[h, z] = r2[h, 0] + r2[h, 1] + r2[h, 2] + r2[h, 3]
        for d in range(1, NZ):
            send(zb.at[h, z], zb.at[h, z], z_s.at[h, d], z_r.at[h, z], along_z(d))

    for d in range(1, NZ):
        source = (z + d) % NZ
        arrived(gz.at[source], gz_r.at[source])
    packed = gz[0]
    for i in range(1, NZ):
        packed = packed + gz[i]
    gram = jnp.concatenate([packed] + [pltpu.roll(packed, 128 - RANK * b, 1) for b in range(1, 4)], axis=0)
    inverse = inverse_factor(gram)[:, :RANK]
    ov[...] = full_dot(inverse, left, ((1,), (0,)))
    ortho_copy = pltpu.make_async_copy(ov, ortho_out, out_sem.at[2])
    ortho_copy.start()

    base = c * 32
    for h in range(2):
        for d in range(1, NZ):
            source = (z + d) % NZ
            arrived(zb.at[h, source], z_r.at[h, source])
        value = zb[h, 0]
        for i in range(1, NZ):
            value = value + zb[h, i]
        block = base + h * 16 + first[h] * 4 + second[h]
        nb[block] = full_dot(inverse, value, ((1,), (0,)))
        for d in range(1, 4):
            send(nb.at[block], nb.at[block], a2_s.at[h, d], a2_r.at[h, second[h]], along_second[h](d))
    for h in range(2):
        mine = base + h * 16 + first[h] * 4
        for d in range(1, 4):
            source = (second[h] + d) % 4
            arrived(nb.at[mine + source], a2_r.at[h, source])
        rows = pl.ds(mine, 4)
        for d in range(1, 4):
            send(nb.at[rows], nb.at[rows], a1_s.at[h, d], a1_r.at[h, first[h]], along_first[h](d))
        send(nb.at[rows], nb.at[rows], ac_s.at[h, 0], ac_r.at[h, 0], partner)
    for d in range(1, 4):
        for h in range(2):
            source = (first[h] + d) % 4
            rows = pl.ds(base + h * 16 + source * 4, 4)
            arrived(nb.at[rows], a1_r.at[h, source])
            send(nb.at[rows], nb.at[rows], ac_s.at[h, d], ac_r.at[h, d], partner)
    half = pl.ds(base, 32)
    half_copy = pltpu.make_async_copy(nb.at[half], nb_out.at[half], out_sem.at[0])
    half_copy.start()
    for d in range(4):
        for h in range(2):
            source = (first[h] + d) % 4
            rows = pl.ds((1 - c) * 32 + h * 16 + source * 4, 4)
            arrived(nb.at[rows], ac_r.at[h, d])
    other = pl.ds((1 - c) * 32, 32)
    other_copy = pltpu.make_async_copy(nb.at[other], nb_out.at[other], out_sem.at[1])
    other_copy.start()
    for copy in sent:
        copy.wait_send()
    ortho_copy.wait()
    half_copy.wait()
    other_copy.wait()


def apply_kernel(overflow, grad, error, nb, ortho, update, new_error, basis_out):
    width = grad.shape[1]
    health = 1.0 - overflow[0].astype(F32)
    new_basis = jnp.concatenate([nb[i] for i in range(width // 128)], axis=1)
    basis_out[...] = new_basis
    n1, n2, _ = pieces(new_basis)
    o1, o2, _ = pieces(ortho[...])
    approx = lax.dot_general(
        jnp.concatenate([o1, o1, o2], axis=0),
        jnp.concatenate([n1, n2, n1], axis=0),
        (((0,), (0,)), ((), ())),
        preferred_element_type=F32,
    )
    update[...] = approx.astype(BF16)
    error_value = error[...].astype(F32)
    corrected = grad[...].astype(F32) + error_value
    new_error[...] = jnp.where(health > 0.5, corrected - approx, error_value).astype(BF16)


def on_device(grad_out, error_out, basis_out, overflow):
    grad, error = grad_out[0], error_out[0]
    any_spec = pl.BlockSpec(memory_space=pl.ANY)
    dma = pltpu.SemaphoreType.DMA
    vmem = lambda *shape: pltpu.VMEM(shape, F32)
    block = (RANK, 128)
    nb, ortho = pl.pallas_call(
        reduce_kernel,
        out_shape=[jax.ShapeDtypeStruct((64, RANK, 128), F32), jax.ShapeDtypeStruct((RANK, ROWS), F32)],
        in_specs=[any_spec, any_spec, any_spec, pl.BlockSpec(memory_space=pltpu.SMEM)],
        out_specs=[any_spec, any_spec],
        scratch_shapes=[
            pltpu.VMEM((2 * ROWS, D), BF16),
            vmem(RANK, D),
            vmem(2, RANK + 8, 128),
            vmem(NY, RANK + 8, 128),
            vmem(NX, 8, 128),
            vmem(NZ, 8, 128),
            vmem(32, *block),
            vmem(32, *block),
            vmem(32, *block),
            vmem(2, 4, 4, *block),
            vmem(2, 4, *block),
            vmem(2, 4, *block),
            vmem(2, NZ, *block),
            vmem(64, *block),
            vmem(*block),
            dma((3, CHUNKS)),
            dma((1,)), dma((1,)),
            dma((NY,)), dma((NY,)),
            dma((NX,)), dma((NX,)),
            dma((NZ,)), dma((NZ,)),
            dma((8,)), dma((8,)),
            dma((2, 4)), dma((2, 4)),
            dma((2, 4)), dma((2, 4)),
            dma((2, NZ)), dma((2, NZ)),
            dma((2, 4)), dma((2, 4)),
            dma((2, 4)), dma((2, 4)),
            dma((2, 4)), dma((2, 4)),
            dma((3,)),
        ],
        compiler_params=pltpu.CompilerParams(collective_id=0, has_side_effects=True, vmem_limit_bytes=40 << 20),
        name="reduce",
    )(grad, error, basis_out.T, overflow)

    width = 1024
    wide = pl.BlockSpec((ROWS, width), lambda i: (0, i))
    update, new_error, new_basis = pl.pallas_call(
        apply_kernel,
        grid=(D // width,),
        out_shape=[
            jax.ShapeDtypeStruct((ROWS, D), BF16),
            jax.ShapeDtypeStruct((ROWS, D), BF16),
            jax.ShapeDtypeStruct((RANK, D), F32),
        ],
        in_specs=[
            pl.BlockSpec(memory_space=pltpu.SMEM),
            wide,
            wide,
            pl.BlockSpec((width // 128, RANK, 128), lambda i: (i, 0, 0)),
            pl.BlockSpec((RANK, ROWS), lambda i: (0, 0)),
        ],
        out_specs=[wide, wide, pl.BlockSpec((RANK, width), lambda i: (0, i))],
        compiler_params=pltpu.CompilerParams(vmem_limit_bytes=24 << 20),
        name="apply",
    )(overflow, grad, error, nb, ortho)
    return update, new_error[None], new_basis.T


def solution(mesh):
    return jax.shard_map(
        on_device,
        mesh=mesh,
        in_specs=(P("rep", "shard", None), P("rep", "shard", None), P(), P("rep")),
        out_specs=(P("shard", None), P("rep", "shard", None), P()),
        check_vma=False,
    )
```

```python
import functools

import jax
import jax.numpy as jnp
from jax import lax
from jax.experimental import pallas as pl
from jax.experimental.pallas import tpu as pltpu
from jax.sharding import PartitionSpec as P

MESH = pl.DeviceIdType.MESH
F32, BF16 = jnp.float32, jnp.bfloat16
D, RANK, ROWS = 8192, 32, 128
CHUNKS, AHEAD = 8, 3
CHUNK = D // CHUNKS
NY, NX, NZ = 4, 4, 8
WIDTH = 1024


def pieces(value):
    first = value.astype(BF16)
    rest = value - first.astype(F32)
    second = rest.astype(BF16)
    third = (rest - second.astype(F32)).astype(BF16)
    return first, second, third


def full_dot(a, b, dims):
    return lax.dot_general(a, b, (dims, ((), ())), precision=lax.Precision.HIGHEST, preferred_element_type=F32)


def inverse_factor(gram):
    row = lax.broadcasted_iota(jnp.int32, (RANK, 128), 0)
    lane = lax.broadcasted_iota(jnp.int32, (RANK, 128), 1)
    diagonal = row == lane
    trace = jnp.sum(jnp.where(diagonal, gram, 0.0), axis=(0, 1), keepdims=True)
    shift = 1e-05 * (trace / RANK)
    work = jnp.where(lane < RANK, gram, 0.0) + jnp.where(diagonal, shift, 0.0)
    work = work + jnp.where(lane - RANK == row, 1.0, 0.0)
    for j in range(RANK - 1):
        column = jnp.broadcast_to(work[:, j : j + 1], (RANK, 128))
        scaled = work[j : j + 1, :] / column[j : j + 1, :]
        work = work - jnp.where(row > j, column, 0.0) * scaled
    pivots = jnp.sum(jnp.where(diagonal, work, 0.0), axis=1, keepdims=True)
    inverse = work * lax.rsqrt(pivots)
    return pltpu.roll(inverse, 128 - RANK, 1)


def reduce_kernel(
    grad_hbm, error_hbm, basis_hbm, overflow, nb, ortho, ge,
    bt, lc, ly, gx, gz, sp, rc, t1, r1, t2, r2, zb,
    in_sem, lc_s, lc_r, ly_s, ly_r, gx_s, gx_r, gz_s, gz_r, rc_s, rc_r,
    p1_s, p1_r, p2_s, p2_r, z_s, z_r, a2_s, a2_r, a1_s, a1_r, ac_s, ac_r, ag_s, ag_r,
):
    rep, shard = lax.axis_index("rep"), lax.axis_index("shard")
    y, c = rep // 2, rep % 2
    x, z = shard // NZ, shard % NZ

    def at(y_, c_, x_, z_):
        return (y_ * 2 + c_, x_ * NZ + z_)

    partner = at(y, 1 - c, x, z)

    def along_y(d):
        return at((y + d) % NY, c, x, z)

    def along_x(d):
        return at(y, c, (x + d) % NX, z)

    def along_z(d):
        return at(y, c, x, (z + d) % NZ)

    def remote(src, dst, send, recv, device):
        return pltpu.make_async_remote_copy(
            src_ref=src, dst_ref=dst, send_sem=send, recv_sem=recv, device_id=device, device_id_type=MESH
        )

    sent = []

    def send(src, dst, send_sem, recv_sem, device):
        copy = remote(src, dst, send_sem, recv_sem, device)
        copy.start()
        sent.append(copy)

    def arrived(dst, recv_sem):
        remote(dst, dst, lc_s.at[0], recv_sem, partner).wait_recv()

    def load(k):
        cols = pl.ds(k * CHUNK, CHUNK)
        return [
            pltpu.make_async_copy(basis_hbm.at[:, cols], bt.at[:, cols], in_sem.at[0, k]),
            pltpu.make_async_copy(grad_hbm.at[:, cols], ge.at[pl.ds(0, ROWS), cols], in_sem.at[1, k]),
            pltpu.make_async_copy(error_hbm.at[:, cols], ge.at[pl.ds(ROWS, ROWS), cols], in_sem.at[2, k]),
        ]

    loads = [load(k) for k in range(CHUNKS)]
    for k in range(AHEAD):
        for copy in loads[k]:
            copy.start()

    barrier = pltpu.get_barrier_semaphore()
    others = [partner]
    others += [along_y(d) for d in range(1, NY)] + [along_x(d) for d in range(1, NX)]
    others += [along_z(d) for d in range(1, NZ)]
    for other in others:
        pl.semaphore_signal(barrier, inc=1, device_id=other, device_id_type=MESH)

    health = jnp.full((8, 128), 1.0 - overflow[0].astype(F32), F32)
    acc = jnp.zeros((3 * RANK, 2 * ROWS), F32)
    for k in range(CHUNKS):
        for copy in loads[k]:
            copy.wait()
        if k + AHEAD < CHUNKS:
            for copy in loads[k + AHEAD]:
                copy.start()
        cols = pl.ds(k * CHUNK, CHUNK)
        basis = jnp.concatenate(pieces(bt[:, cols]), axis=0)
        acc += lax.dot_general(basis, ge[:, cols], (((1,), (1,)), ((), ())), preferred_element_type=F32)
    both = acc[:RANK] + acc[RANK : 2 * RANK] + acc[2 * RANK :]
    lc[0, :RANK] = (both[:, :ROWS] + both[:, ROWS:]) * health[:1]
    lc[0, RANK:] = health

    pl.semaphore_wait(barrier, len(others))

    send(lc.at[0], lc.at[1], lc_s.at[0], lc_r.at[0], partner)
    arrived(lc.at[1], lc_r.at[0])
    ly[y] = lc[0] + lc[1]
    for d in range(1, NY):
        send(ly.at[y], ly.at[y], ly_s.at[d], ly_r.at[y], along_y(d))
    for d in range(1, NY):
        source = (y + d) % NY
        arrived(ly.at[source], ly_r.at[source])
    total = ly[0] + ly[1] + ly[2] + ly[3]
    kept = total[RANK : RANK + 1]
    left = total[:RANK] / kept

    gram = full_dot(left, jnp.concatenate([left] * 4, axis=0), ((1,), (1,)))
    lane_group = lax.broadcasted_iota(jnp.int32, (8, 128), 1) // RANK
    packed = gram[:8]
    for b in range(1, 4):
        packed = jnp.where(lane_group == b, gram[8 * b : 8 * b + 8], packed)
    gx[x] = packed
    for d in range(1, NX):
        send(gx.at[x], gx.at[x], gx_s.at[d], gx_r.at[x], along_x(d))

    weighted = jnp.concatenate(pieces(left * (health[:1] / kept)), axis=0)
    weighted = jnp.concatenate([weighted, weighted], axis=1)

    def product(block):
        cols = pl.ds(pl.multiple_of(block * 128, 512), 512)
        out = lax.dot_general(weighted, ge[:, cols], (((1,), (0,)), ((), ())), preferred_element_type=F32)
        return out[:RANK] + out[RANK : 2 * RANK] + out[2 * RANK :]

    first = (x, y)
    second = (y, x)
    along_first = (along_x, along_y)
    along_second = (along_y, along_x)
    order = [(d, h) for h in range(2) for d in (1, 2, 3, 0)]
    for i, (d, h) in enumerate(order):
        group = h * 16 + ((first[h] + d) % 4) * 4
        theirs = (1 - c) * 32 + group
        value = product(theirs)
        for q in range(4):
            sp[group + q] = value[:, q * 128 : (q + 1) * 128]
        send(sp.at[pl.ds(group, 4)], rc.at[pl.ds(group, 4)], rc_s.at[i], rc_r.at[i], partner)
    for i, (d, h) in enumerate(order):
        p = (first[h] + d) % 4
        group = h * 16 + p * 4
        value = product(c * 32 + group)
        arrived(rc.at[pl.ds(group, 4)], rc_r.at[i])
        if d == 0:
            for q in range(4):
                r1[h, p, q] = value[:, q * 128 : (q + 1) * 128] + rc[group + q]
        else:
            for q in range(4):
                t1[group + q] = value[:, q * 128 : (q + 1) * 128] + rc[group + q]
            send(t1.at[pl.ds(group, 4)], r1.at[h, first[h]], p1_s.at[h, d], p1_r.at[h, first[h]], along_first[h](d))

    for d in range(1, NX):
        source = (x + d) % NX
        arrived(gx.at[source], gx_r.at[source])
    gz[z] = gx[0] + gx[1] + gx[2] + gx[3]
    for d in range(1, NZ):
        send(gz.at[z], gz.at[z], gz_s.at[d], gz_r.at[z], along_z(d))

    for h in range(2):
        for d in range(1, 4):
            source = (first[h] + d) % 4
            arrived(r1.at[h, source], p1_r.at[h, source])
        for q in range(4):
            t2[h, q] = r1[h, 0, q] + r1[h, 1, q] + r1[h, 2, q] + r1[h, 3, q]
        for d in range(1, 4):
            q = (second[h] + d) % 4
            send(t2.at[h, q], r2.at[h, second[h]], p2_s.at[h, d], p2_r.at[h, second[h]], along_second[h](d))
        r2[h, second[h]] = t2[h, second[h]]
    for h in range(2):
        for d in range(1, 4):
            source = (second[h] + d) % 4
            arrived(r2.at[h, source], p2_r.at[h, source])
        zb[h, z] = r2[h, 0] + r2[h, 1] + r2[h, 2] + r2[h, 3]
        for d in range(1, NZ):
            send(zb.at[h, z], zb.at[h, z], z_s.at[h, d], z_r.at[h, z], along_z(d))

    for d in range(1, NZ):
        source = (z + d) % NZ
        arrived(gz.at[source], gz_r.at[source])
    packed = gz[0]
    for i in range(1, NZ):
        packed = packed + gz[i]
    gram = jnp.concatenate([packed] + [pltpu.roll(packed, 128 - RANK * b, 1) for b in range(1, 4)], axis=0)
    inverse = inverse_factor(gram)[:, :RANK]
    ortho[...] = full_dot(inverse, left, ((1,), (0,)))

    def forward(h, p, q):
        block = c * 32 + h * 16 + p * 4 + q
        for d in (1, 3, 2):
            send(nb.at[block], nb.at[block], a1_s.at[h, d, q], a1_r.at[h, p, q], along_first[h](d))
        send(nb.at[block], nb.at[block], ac_s.at[h, 0, q], ac_r.at[h, p, q], partner)

    for h in range(2):
        for d in range(1, NZ):
            source = (z + d) % NZ
            arrived(zb.at[h, source], z_r.at[h, source])
        value = zb[h, 0]
        for i in range(1, NZ):
            value = value + zb[h, i]
        block = c * 32 + h * 16 + first[h] * 4 + second[h]
        nb[block] = full_dot(inverse, value, ((1,), (0,)))
        for d in (1, 3, 2):
            send(nb.at[block], nb.at[block], a2_s.at[h, d], a2_r.at[h, second[h]], along_second[h](d))
        forward(h, first[h], second[h])
    for d in (1, 3, 2):
        for h in range(2):
            q = (second[h] + d) % 4
            block = c * 32 + h * 16 + first[h] * 4 + q
            arrived(nb.at[block], a2_r.at[h, q])
            forward(h, first[h], q)
    for d in (1, 3, 2):
        for h in range(2):
            p = (first[h] + d) % 4
            for k in range(4):
                q = (second[h] + (0, 1, 3, 2)[k]) % 4
                block = c * 32 + h * 16 + p * 4 + q
                arrived(nb.at[block], a1_r.at[h, p, q])
            rows = pl.ds(c * 32 + h * 16 + p * 4, 4)
            send(nb.at[rows], nb.at[rows], ag_s.at[h, d], ag_r.at[h, p], partner)
    for h in range(2):
        theirs = (1 - c) * 32 + h * 16
        for q in range(4):
            arrived(nb.at[theirs + first[h] * 4 + q], ac_r.at[h, first[h], q])
        for d in (1, 3, 2):
            p = (first[h] + d) % 4
            arrived(nb.at[pl.ds(theirs + p * 4, 4)], ag_r.at[h, p])
    for copy in sent:
        copy.wait_send()


def apply_kernel(overflow, ge, nb, ortho, update_hbm, error_hbm, basis_hbm, update, new_error, basis, sem):
    health = 1.0 - overflow[0].astype(F32)
    o1, o2, _ = pieces(ortho[...])
    ortho_pieces = jnp.concatenate([o1, o1, o2], axis=0)
    copies = []
    for k in range(D // WIDTH):
        cols = pl.ds(k * WIDTH, WIDTH)
        count = WIDTH // 128
        new_basis = jnp.concatenate([nb[k * count + i] for i in range(count)], axis=1)
        basis[:, cols] = new_basis
        n1, n2, _ = pieces(new_basis)
        approx = lax.dot_general(
            ortho_pieces,
            jnp.concatenate([n1, n2, n1], axis=0),
            (((0,), (0,)), ((), ())),
            preferred_element_type=F32,
        )
        update[:, cols] = approx.astype(BF16)
        error_value = ge[ROWS:, cols].astype(F32)
        corrected = ge[:ROWS, cols].astype(F32) + error_value
        new_error[:, cols] = jnp.where(health > 0.5, corrected - approx, error_value).astype(BF16)
        for i, (value, out) in enumerate(((basis, basis_hbm), (update, update_hbm), (new_error, error_hbm))):
            copy = pltpu.make_async_copy(value.at[:, cols], out.at[:, cols], sem.at[i, k])
            copy.start()
            copies.append(copy)
    for copy in copies:
        copy.wait()


def on_device(grad_out, error_out, basis_out, overflow):
    grad, error = grad_out[0], error_out[0]
    hbm = pl.BlockSpec(memory_space=pltpu.MemorySpace.HBM)
    smem, whole = pl.BlockSpec(memory_space=pltpu.SMEM), pl.BlockSpec(memory_space=pltpu.VMEM)
    dma = pltpu.SemaphoreType.DMA
    vmem = lambda *shape: pltpu.VMEM(shape, F32)
    block = (RANK, 128)
    operands = [pltpu.with_memory_space_constraint(a, pltpu.HBM) for a in (grad, error, basis_out.T)]
    nb, ortho, ge = pl.pallas_call(
        reduce_kernel,
        out_shape=[
            vmem(64, *block),
            vmem(RANK, ROWS),
            pltpu.VMEM((2 * ROWS, D), BF16),
        ],
        in_specs=[hbm, hbm, hbm, smem],
        out_specs=[whole, whole, whole],
        scratch_shapes=[
            vmem(RANK, D),
            vmem(2, RANK + 8, 128),
            vmem(NY, RANK + 8, 128),
            vmem(NX, 8, 128),
            vmem(NZ, 8, 128),
            vmem(32, *block),
            vmem(32, *block),
            vmem(32, *block),
            vmem(2, 4, 4, *block),
            vmem(2, 4, *block),
            vmem(2, 4, *block),
            vmem(2, NZ, *block),
            dma((3, CHUNKS)),
            dma((1,)), dma((1,)),
            dma((NY,)), dma((NY,)),
            dma((NX,)), dma((NX,)),
            dma((NZ,)), dma((NZ,)),
            dma((8,)), dma((8,)),
            dma((2, 4)), dma((2, 4)),
            dma((2, 4)), dma((2, 4)),
            dma((2, NZ)), dma((2, NZ)),
            dma((2, 4)), dma((2, 4)),
            dma((2, 4, 4)), dma((2, 4, 4)),
            dma((2, 1, 4)), dma((2, 4, 4)),
            dma((2, 4)), dma((2, 4)),
        ],
        compiler_params=pltpu.CompilerParams(collective_id=0, has_side_effects=True, vmem_limit_bytes=32 << 20),
        name="reduce",
    )(*operands, overflow)

    update, new_error, new_basis = pl.pallas_call(
        apply_kernel,
        out_shape=[
            jax.ShapeDtypeStruct((ROWS, D), BF16),
            jax.ShapeDtypeStruct((ROWS, D), BF16),
            jax.ShapeDtypeStruct((RANK, D), F32),
        ],
        in_specs=[smem, whole, whole, whole],
        out_specs=[hbm, hbm, hbm],
        scratch_shapes=[
            pltpu.VMEM((ROWS, D), BF16), pltpu.VMEM((ROWS, D), BF16), vmem(RANK, D), dma((3, D // WIDTH))
        ],
        compiler_params=pltpu.CompilerParams(vmem_limit_bytes=24 << 20),
        name="apply",
    )(overflow, ge, nb, ortho)
    return update, new_error[None], new_basis.T


def solution(mesh):
    return jax.shard_map(
        on_device,
        mesh=mesh,
        in_specs=(P("rep", "shard", None), P("rep", "shard", None), P(), P("rep")),
        out_specs=(P("shard", None), P("rep", "shard", None), P()),
        check_vma=False,
    )
```

```python
import functools

import jax
import jax.numpy as jnp
from jax import lax
from jax.experimental import pallas as pl
from jax.experimental.pallas import tpu as pltpu
from jax.sharding import PartitionSpec as P

MESH = pl.DeviceIdType.MESH
F32, BF16 = jnp.float32, jnp.bfloat16
D, RANK, ROWS = 8192, 32, 128
HALF, MPARTS = D // 2, 4
NY, NX, NZ = 4, 4, 8
WIDTH = 1024


def pieces(value):
    first = value.astype(BF16)
    rest = value - first.astype(F32)
    second = rest.astype(BF16)
    third = (rest - second.astype(F32)).astype(BF16)
    return first, second, third


def full_dot(a, b, dims):
    return lax.dot_general(a, b, (dims, ((), ())), precision=lax.Precision.HIGHEST, preferred_element_type=F32)


def inverse_factor(gram):
    row = lax.broadcasted_iota(jnp.int32, (RANK, 128), 0)
    lane = lax.broadcasted_iota(jnp.int32, (RANK, 128), 1)
    diagonal = row == lane
    trace = jnp.sum(jnp.where(diagonal, gram, 0.0), axis=(0, 1), keepdims=True)
    shift = 1e-05 * (trace / RANK)
    work = jnp.where(lane < RANK, gram, 0.0) + jnp.where(diagonal, shift, 0.0)
    work = work + jnp.where(lane - RANK == row, 1.0, 0.0)
    for j in range(RANK - 1):
        column = jnp.broadcast_to(work[:, j : j + 1], (RANK, 128))
        scaled = work[j : j + 1, :] / column[j : j + 1, :]
        work = work - jnp.where(row > j, column, 0.0) * scaled
    pivots = jnp.sum(jnp.where(diagonal, work, 0.0), axis=1, keepdims=True)
    inverse = work * lax.rsqrt(pivots)
    return pltpu.roll(inverse, 128 - RANK, 1)


def reduce_kernel(
    grad_hbm, error_hbm, basis_hbm, overflow, nb, ortho, ge,
    bt, hb, mo, mi, mc, ly, gx, gz, t1, r1, t2, r2, zb,
    in_sem, m_r, ly_r, gx_r, gz_r, p1_r, p2_r, z_r, a2_r, a1_r, ac_r, s_sem,
):
    rep, shard = lax.axis_index("rep"), lax.axis_index("shard")
    y, c = rep // 2, rep % 2
    x, z = shard // NZ, shard % NZ

    def at(y_, c_, x_, z_):
        return (y_ * 2 + c_, x_ * NZ + z_)

    partner = at(y, 1 - c, x, z)

    def along_y(d):
        return at((y + d) % NY, c, x, z)

    def along_x(d):
        return at(y, c, (x + d) % NX, z)

    def along_z(d):
        return at(y, c, x, (z + d) % NZ)

    def remote(src, dst, send, recv, device):
        return pltpu.make_async_remote_copy(
            src_ref=src, dst_ref=dst, send_sem=send, recv_sem=recv, device_id=device, device_id_type=MESH
        )

    def send(src, dst, phase, recv_sem, device):
        remote(src, dst, s_sem.at[phase], recv_sem, device).start()

    def arrived(like, recv_sem):
        remote(like, like, s_sem.at[0], recv_sem, partner).wait_recv()

    def all_sent(like, phase):
        remote(like, like, s_sem.at[phase], m_r.at[0], partner).wait_send()

    def blocks(count):
        return nb.at[pl.ds(0, count)]

    halves = [(1 - c) * HALF, c * HALF]
    loads = []
    for i, start in enumerate(halves):
        cols = pl.ds(pl.multiple_of(start, HALF), HALF)
        group = [
            pltpu.make_async_copy(grad_hbm.at[:, cols], ge.at[pl.ds(0, ROWS), cols], in_sem.at[0, i]),
            pltpu.make_async_copy(error_hbm.at[:, cols], ge.at[pl.ds(ROWS, ROWS), cols], in_sem.at[1, i]),
            pltpu.make_async_copy(basis_hbm.at[:, cols], bt.at[:, cols], in_sem.at[2, i]),
        ]
        for copy in group:
            copy.start()
        loads.append(group)

    barrier = pltpu.get_barrier_semaphore()
    replicas = [(2, 0), (2, 1), (1, 0), (3, 0), (1, 1), (3, 1), (0, 1)]
    replicas = [at((y + dy) % NY, (c + dc) % 2, x, z) for dy, dc in replicas]
    others = replicas + [along_x(d) for d in range(1, NX)] + [along_z(d) for d in range(1, NZ)]
    for other in others:
        pl.semaphore_signal(barrier, inc=1, device_id=other, device_id_type=MESH)

    health = jnp.full((8, 128), 1.0 - overflow[0].astype(F32), F32)
    hb[0] = health
    weight = health[:1, :1]

    def corrected(start):
        cols = pl.ds(pl.multiple_of(start, 512), 512)
        return (ge[:ROWS, cols].astype(F32) + ge[ROWS:, cols].astype(F32)) * weight

    def project(start):
        cols = pl.ds(pl.multiple_of(start, 512), 1024)
        basis = jnp.concatenate(pieces(bt[:, cols]), axis=0)
        return lax.dot_general(basis, ge[:, cols], (((1,), (1,)), ((), ())), preferred_element_type=F32)

    for copy in loads[0]:
        copy.wait()
    acc = jnp.zeros((3 * RANK, 2 * ROWS), F32)
    for k in range(HALF // 1024):
        acc += project(halves[0] + k * 1024)
        for i in range(2):
            mo[:, pl.ds(k * 1024 + i * 512, 512)] = corrected(halves[0] + k * 1024 + i * 512)
    pl.semaphore_wait(barrier, len(others))
    send(hb.at[0], hb.at[1], 0, m_r.at[MPARTS], partner)
    for k in range(MPARTS):
        rows = pl.ds(k * (ROWS // MPARTS), ROWS // MPARTS)
        send(mo.at[rows], mi.at[rows], 1, m_r.at[k], partner)
    for copy in loads[1]:
        copy.wait()
    for k in range(HALF // 1024):
        acc += project(halves[1] + k * 1024)
    both = acc[:RANK] + acc[RANK : 2 * RANK] + acc[2 * RANK :]

    ly[rep] = (both[:, :ROWS] + both[:, ROWS:]) * weight
    for other in replicas:
        send(ly.at[rep], ly.at[rep], 2, ly_r.at[0], other)

    for k in range(MPARTS):
        size = ROWS // MPARTS
        rows = pl.ds(k * size, size)
        arrived(mi.at[rows], m_r.at[k])
        for i in range(HALF // 1024):
            own = pl.ds(pl.multiple_of(halves[1] + i * 1024, 1024), 1024)
            cols = pl.ds(i * 1024, 1024)
            value = ge[rows, own].astype(F32) + ge[pl.ds(ROWS + k * size, size), own].astype(F32)
            value = value * weight + mi[rows, cols]
            high = value.astype(BF16)
            mc[rows, cols] = high
            mc[pl.ds(ROWS + k * size, size), cols] = (value - high.astype(F32)).astype(BF16)
    arrived(hb.at[1], m_r.at[MPARTS])
    count = hb[0] + hb[1]

    arrived(ly.at[pl.ds(0, 7)], ly_r.at[0])
    left = ly[0]
    for i in range(1, 8):
        left = left + ly[i]

    weighted = jnp.concatenate(pieces(left), axis=0)
    weighted = jnp.concatenate([weighted, weighted], axis=1)
    first = (x, y)
    second = (y, x)
    along_first = (along_x, along_y)
    along_second = (along_y, along_x)
    for d in (2, 1, 3, 0):
        for h in range(2):
            p = (first[h] + d) % 4
            group = h * 16 + p * 4
            cols = pl.ds(pl.multiple_of(group * 128, 512), 512)
            out = lax.dot_general(weighted, mc[:, cols], (((1,), (0,)), ((), ())), preferred_element_type=F32)
            value = out[:RANK] + out[RANK : 2 * RANK] + out[2 * RANK :]
            for q in range(4):
                part = value[:, q * 128 : (q + 1) * 128]
                if d == 0:
                    r1[h, p, q] = part
                else:
                    t1[group + q] = part
            if d:
                send(t1.at[pl.ds(group, 4)], r1.at[h, first[h]], 3, p1_r.at[h], along_first[h](d))

    gram = full_dot(left, jnp.concatenate([left] * 4, axis=0), ((1,), (1,)))
    lane_group = lax.broadcasted_iota(jnp.int32, (8, 128), 1) // RANK
    packed = gram[:8]
    for b in range(1, 4):
        packed = jnp.where(lane_group == b, gram[8 * b : 8 * b + 8], packed)
    gx[x] = packed
    for d in (2, 1, 3):
        send(gx.at[x], gx.at[x], 4, gx_r.at[0], along_x(d))
    all_sent(hb.at[0], 0)
    all_sent(mo, 1)
    all_sent(blocks(7), 2)
    arrived(gx.at[pl.ds(0, 3)], gx_r.at[0])
    gz[z] = gx[0] + gx[1] + gx[2] + gx[3]
    for d in (4, 3, 5, 2, 6, 1, 7):
        send(gz.at[z], gz.at[z], 5, gz_r.at[0], along_z(d))

    for h in range(2):
        arrived(blocks(12), p1_r.at[h])
        for q in range(4):
            t2[h * 4 + q, :RANK] = r1[h, 0, q] + r1[h, 1, q] + r1[h, 2, q] + r1[h, 3, q]
            t2[h * 4 + q, RANK:] = count
        for d in (2, 1, 3):
            q = (second[h] + d) % 4
            send(t2.at[h * 4 + q], r2.at[h * 4 + second[h]], 6, p2_r.at[h], along_second[h](d))
        r2[h * 4 + second[h]] = t2[h * 4 + second[h]]
    for h in range(2):
        arrived(r2.at[pl.ds(0, 3)], p2_r.at[h])
    for h in range(2):
        zb[z, h] = r2[h * 4, :RANK] + r2[h * 4 + 1, :RANK] + r2[h * 4 + 2, :RANK] + r2[h * 4 + 3, :RANK]
    for d in (4, 3, 5, 2, 6, 1, 7):
        send(zb.at[z], zb.at[z], 7, z_r.at[0], along_z(d))
    kept = r2[0, RANK:] + r2[1, RANK:] + r2[2, RANK:] + r2[3, RANK:]

    all_sent(blocks(24), 3)
    all_sent(gx.at[pl.ds(0, 3)], 4)
    all_sent(gz.at[pl.ds(0, 7)], 5)
    arrived(gz.at[pl.ds(0, 7)], gz_r.at[0])
    packed = gz[0]
    for i in range(1, NZ):
        packed = packed + gz[i]
    gram = jnp.concatenate([packed] + [pltpu.roll(packed, 128 - RANK * b, 1) for b in range(1, 4)], axis=0)
    inverse = inverse_factor(gram)[:, :RANK]
    ortho[...] = full_dot(inverse, left, ((1,), (0,)))
    all_sent(r2.at[pl.ds(0, 6)], 6)

    arrived(zb.at[pl.ds(0, 7)], z_r.at[0])
    base = c * 32
    for h in range(2):
        value = zb[0, h]
        for i in range(1, NZ):
            value = value + zb[i, h]
        block = base + h * 16 + first[h] * 4 + second[h]
        nb[block] = full_dot(inverse, value, ((1,), (0,))) / kept[:1]
        for d in (2, 1, 3):
            send(nb.at[block], nb.at[block], 8, a2_r.at[h], along_second[h](d))
    for h in range(2):
        arrived(blocks(3), a2_r.at[h])
        rows = pl.ds(base + h * 16 + first[h] * 4, 4)
        for d in (2, 1, 3):
            send(nb.at[rows], nb.at[rows], 9, a1_r.at[h, first[h]], along_first[h](d))
        send(nb.at[rows], nb.at[rows], 10, ac_r.at[0], partner)
    all_sent(blocks(14), 7)
    all_sent(blocks(6), 8)
    for d in (1, 3, 2):
        for h in range(2):
            p = (first[h] + d) % 4
            rows = pl.ds(base + h * 16 + p * 4, 4)
            arrived(nb.at[rows], a1_r.at[h, p])
            send(nb.at[rows], nb.at[rows], 10, ac_r.at[0], partner)
    all_sent(blocks(24), 9)
    arrived(blocks(32), ac_r.at[0])
    all_sent(blocks(32), 10)


def apply_kernel(overflow, ge, nb, ortho, update_hbm, error_hbm, basis_hbm, update, new_error, basis, sem):
    health = 1.0 - overflow[0].astype(F32)
    o1, o2, _ = pieces(ortho[...])
    ortho_pieces = jnp.concatenate([o1, o1, o2], axis=0)
    copies = []
    for k in range(D // WIDTH):
        cols = pl.ds(k * WIDTH, WIDTH)
        count = WIDTH // 128
        new_basis = jnp.concatenate([nb[k * count + i] for i in range(count)], axis=1)
        basis[:, cols] = new_basis
        n1, n2, _ = pieces(new_basis)
        approx = lax.dot_general(
            ortho_pieces,
            jnp.concatenate([n1, n2, n1], axis=0),
            (((0,), (0,)), ((), ())),
            preferred_element_type=F32,
        )
        update[:, cols] = approx.astype(BF16)
        error_value = ge[ROWS:, cols].astype(F32)
        corrected = ge[:ROWS, cols].astype(F32) + error_value
        new_error[:, cols] = jnp.where(health > 0.5, corrected - approx, error_value).astype(BF16)
        for i, (value, out) in enumerate(((basis, basis_hbm), (update, update_hbm), (new_error, error_hbm))):
            copy = pltpu.make_async_copy(value.at[:, cols], out.at[:, cols], sem.at[i, k])
            copy.start()
            copies.append(copy)
    for copy in copies:
        copy.wait()


def on_device(grad_out, error_out, basis_out, overflow):
    grad, error = grad_out[0], error_out[0]
    hbm = pl.BlockSpec(memory_space=pltpu.MemorySpace.HBM)
    smem, whole = pl.BlockSpec(memory_space=pltpu.SMEM), pl.BlockSpec(memory_space=pltpu.VMEM)
    dma = pltpu.SemaphoreType.DMA
    vmem = lambda *shape: pltpu.VMEM(shape, F32)
    block = (RANK, 128)
    operands = [pltpu.with_memory_space_constraint(a, pltpu.HBM) for a in (grad, error, basis_out.T)]
    nb, ortho, ge = pl.pallas_call(
        reduce_kernel,
        out_shape=[
            vmem(64, *block),
            vmem(RANK, ROWS),
            pltpu.VMEM((2 * ROWS, D), BF16),
        ],
        in_specs=[hbm, hbm, hbm, smem],
        out_specs=[whole, whole, whole],
        scratch_shapes=[
            vmem(RANK, D),
            vmem(2, 8, 128),
            vmem(ROWS, HALF),
            vmem(ROWS, HALF),
            pltpu.VMEM((2 * ROWS, HALF), BF16),
            vmem(8, *block),
            vmem(NX, 8, 128),
            vmem(NZ, 8, 128),
            vmem(32, *block),
            vmem(2, 4, 4, *block),
            vmem(8, RANK + 8, 128),
            vmem(8, RANK + 8, 128),
            vmem(NZ, 2, *block),
            dma((3, 2)),
            dma((MPARTS + 1,)),
            dma((1,)),
            dma((1,)),
            dma((1,)),
            dma((2,)),
            dma((2,)),
            dma((1,)),
            dma((2,)),
            dma((2, 4)),
            dma((1,)),
            dma((11,)),
        ],
        compiler_params=pltpu.CompilerParams(collective_id=0, has_side_effects=True, vmem_limit_bytes=32 << 20),
        name="reduce",
    )(*operands, overflow)

    update, new_error, new_basis = pl.pallas_call(
        apply_kernel,
        out_shape=[
            jax.ShapeDtypeStruct((ROWS, D), BF16),
            jax.ShapeDtypeStruct((ROWS, D), BF16),
            jax.ShapeDtypeStruct((RANK, D), F32),
        ],
        in_specs=[smem, whole, whole, whole],
        out_specs=[hbm, hbm, hbm],
        scratch_shapes=[
            pltpu.VMEM((ROWS, D), BF16), pltpu.VMEM((ROWS, D), BF16), vmem(RANK, D), dma((3, D // WIDTH))
        ],
        compiler_params=pltpu.CompilerParams(vmem_limit_bytes=24 << 20),
        name="apply",
    )(overflow, ge, nb, ortho)
    return update, new_error[None], new_basis.T


def solution(mesh):
    return jax.shard_map(
        on_device,
        mesh=mesh,
        in_specs=(P("rep", "shard", None), P("rep", "shard", None), P(), P("rep")),
        out_specs=(P("shard", None), P("rep", "shard", None), P()),
        check_vma=False,
    )
```

```python
import functools

import jax
import jax.numpy as jnp
from jax import lax
from jax.experimental import pallas as pl
from jax.experimental.pallas import tpu as pltpu
from jax.sharding import PartitionSpec as P

MESH = pl.DeviceIdType.MESH
F32, BF16 = jnp.float32, jnp.bfloat16
D, RANK, ROWS = 8192, 32, 128
HALF, MPARTS = D // 2, 4
NY, NX, NZ = 4, 4, 8
WIDTH = 1024
WAITS = sorted(((i, j) for i in range(4) for j in range(4) if i or j), key=lambda d: (min(d[0], 4 - d[0]) + min(d[1], 4 - d[1]), d))


def pieces(value):
    first = value.astype(BF16)
    rest = value - first.astype(F32)
    second = rest.astype(BF16)
    third = (rest - second.astype(F32)).astype(BF16)
    return first, second, third


def full_dot(a, b, dims):
    return lax.dot_general(a, b, (dims, ((), ())), precision=lax.Precision.HIGHEST, preferred_element_type=F32)


def inverse_factor(gram):
    row = lax.broadcasted_iota(jnp.int32, (RANK, 128), 0)
    lane = lax.broadcasted_iota(jnp.int32, (RANK, 128), 1)
    diagonal = row == lane
    trace = jnp.sum(jnp.where(diagonal, gram, 0.0), axis=(0, 1), keepdims=True)
    shift = 1e-05 * (trace / RANK)
    work = jnp.where(lane < RANK, gram, 0.0) + jnp.where(diagonal, shift, 0.0)
    work = work + jnp.where(lane - RANK == row, 1.0, 0.0)
    for j in range(RANK - 1):
        column = jnp.broadcast_to(work[:, j : j + 1], (RANK, 128))
        scaled = work[j : j + 1, :] / column[j : j + 1, :]
        work = work - jnp.where(row > j, column, 0.0) * scaled
    pivots = jnp.sum(jnp.where(diagonal, work, 0.0), axis=1, keepdims=True)
    inverse = work * lax.rsqrt(pivots)
    return pltpu.roll(inverse, 128 - RANK, 1)


def reduce_kernel(
    grad_hbm, error_hbm, basis_hbm, overflow, nb, ortho, ge,
    bt, hb, hs, mo, mi, mc, ly, gx, gz, t1, r1, t2, r2, zb,
    in_sem, m_r, ly_r, hs_r, gx_r, gz_r, p1_r, p2_r, z_r, a_r, ac_r, s_sem,
):
    rep, shard = lax.axis_index("rep"), lax.axis_index("shard")
    y, c = rep // 2, rep % 2
    x, z = shard // NZ, shard % NZ

    def at(y_, c_, x_, z_):
        return (y_ * 2 + c_, x_ * NZ + z_)

    partner = at(y, 1 - c, x, z)

    def across(dx, dy):
        return at((y + dy) % NY, c, (x + dx) % NX, z)

    def slot(dx, dy):
        return (x + dx) % NX * NY + (y + dy) % NY

    def along_z(d):
        return at(y, c, x, (z + d) % NZ)

    def remote(src, dst, send, recv, device):
        return pltpu.make_async_remote_copy(
            src_ref=src, dst_ref=dst, send_sem=send, recv_sem=recv, device_id=device, device_id_type=MESH
        )

    def send(src, dst, phase, recv_sem, device):
        remote(src, dst, s_sem.at[phase], recv_sem, device).start()

    def arrived(like, recv_sem):
        remote(like, like, s_sem.at[0], recv_sem, partner).wait_recv()

    def all_sent(like, phase):
        remote(like, like, s_sem.at[phase], m_r.at[0], partner).wait_send()

    def blocks(count):
        return t1.at[pl.ds(0, count)]

    halves = [(1 - c) * HALF, c * HALF]
    loads = []
    for i, start in enumerate(halves):
        cols = pl.ds(pl.multiple_of(start, HALF), HALF)
        group = [
            pltpu.make_async_copy(grad_hbm.at[:, cols], ge.at[pl.ds(0, ROWS), cols], in_sem.at[0, i]),
            pltpu.make_async_copy(error_hbm.at[:, cols], ge.at[pl.ds(ROWS, ROWS), cols], in_sem.at[1, i]),
            pltpu.make_async_copy(basis_hbm.at[:, cols], bt.at[:, cols], in_sem.at[2, i]),
        ]
        for copy in group:
            copy.start()
        loads.append(group)

    barrier = pltpu.get_barrier_semaphore()
    replicas = [(2, 0), (2, 1), (1, 0), (3, 0), (1, 1), (3, 1), (0, 1)]
    replicas = [at((y + dy) % NY, (c + dc) % 2, x, z) for dy, dc in replicas]
    plane = [(dx, dy) for dx in (2, 1, 3, 0) for dy in (2, 1, 3, 0)]
    others = replicas + [across(dx, dy) for dx, dy in plane if dx] + [along_z(d) for d in range(1, NZ)]
    for other in others:
        pl.semaphore_signal(barrier, inc=1, device_id=other, device_id_type=MESH)

    health = jnp.full((8, 128), 1.0 - overflow[0].astype(F32), F32)
    hb[0] = health
    weight = health[:1, :1]

    def corrected(start):
        cols = pl.ds(pl.multiple_of(start, 512), 512)
        return (ge[:ROWS, cols].astype(F32) + ge[ROWS:, cols].astype(F32)) * weight

    def project(start):
        cols = pl.ds(pl.multiple_of(start, 512), 1024)
        basis = jnp.concatenate(pieces(bt[:, cols]), axis=0)
        return lax.dot_general(basis, ge[:, cols], (((1,), (1,)), ((), ())), preferred_element_type=F32)

    for copy in loads[0]:
        copy.wait()
    acc = jnp.zeros((3 * RANK, 2 * ROWS), F32)
    for k in range(HALF // 1024):
        acc += project(halves[0] + k * 1024)
        for i in range(2):
            mo[:, pl.ds(k * 1024 + i * 512, 512)] = corrected(halves[0] + k * 1024 + i * 512)
    pl.semaphore_wait(barrier, len(others))
    send(hb.at[0], hb.at[1], 0, m_r.at[MPARTS], partner)
    for k in range(MPARTS):
        rows = pl.ds(k * (ROWS // MPARTS), ROWS // MPARTS)
        send(mo.at[rows], mi.at[rows], 1, m_r.at[k], partner)
    for copy in loads[1]:
        copy.wait()
    for k in range(HALF // 1024):
        acc += project(halves[1] + k * 1024)
    both = acc[:RANK] + acc[RANK : 2 * RANK] + acc[2 * RANK :]

    ly[rep] = (both[:, :ROWS] + both[:, ROWS:]) * weight
    for other in replicas:
        send(ly.at[rep], ly.at[rep], 2, ly_r.at[0], other)

    for k in range(MPARTS):
        size = ROWS // MPARTS
        rows = pl.ds(k * size, size)
        arrived(mi.at[rows], m_r.at[k])
        for i in range(HALF // 1024):
            own = pl.ds(pl.multiple_of(halves[1] + i * 1024, 1024), 1024)
            cols = pl.ds(i * 1024, 1024)
            value = ge[rows, own].astype(F32) + ge[pl.ds(ROWS + k * size, size), own].astype(F32)
            value = value * weight + mi[rows, cols]
            high = value.astype(BF16)
            mc[rows, cols] = high
            mc[pl.ds(ROWS + k * size, size), cols] = (value - high.astype(F32)).astype(BF16)
    arrived(hb.at[1], m_r.at[MPARTS])
    hs[y] = hb[0] + hb[1]
    for d in (2, 1, 3):
        send(hs.at[y], hs.at[y], 6, hs_r.at[0], across(0, d))

    arrived(ly.at[pl.ds(0, 7)], ly_r.at[0])
    left = ly[0]
    for i in range(1, 8):
        left = left + ly[i]

    gram = full_dot(left, jnp.concatenate([left] * 4, axis=0), ((1,), (1,)))
    lane_group = lax.broadcasted_iota(jnp.int32, (8, 128), 1) // RANK
    packed = gram[:8]
    for b in range(1, 4):
        packed = jnp.where(lane_group == b, gram[8 * b : 8 * b + 8], packed)
    gx[x] = packed
    for d in (2, 1, 3):
        send(gx.at[x], gx.at[x], 4, gx_r.at[0], across(d, 0))
    weighted = jnp.concatenate(pieces(left), axis=0)
    weighted = jnp.concatenate([weighted, weighted], axis=1)
    first = (x, y)
    second = (y, x)
    for d in (2, 1, 3, 0):
        for h in range(2):
            p = (first[h] + d) % 4
            group = [h * 16 + (p * 4 + q, q * 4 + p)[h] for q in range(4)]
            if h:
                rows = jnp.concatenate([mc[:, pl.ds(pl.multiple_of(b * 128, 128), 128)] for b in group], axis=1)
            else:
                rows = mc[:, pl.ds(pl.multiple_of(group[0] * 128, 512), 512)]
            out = lax.dot_general(weighted, rows, (((1,), (0,)), ((), ())), preferred_element_type=F32)
            value = out[:RANK] + out[RANK : 2 * RANK] + out[2 * RANK :]
            for q in range(4):
                part = value[:, q * 128 : (q + 1) * 128]
                if d == 0:
                    r1[h, p, q] = part
                else:
                    t1[h * 16 + p * 4 + q] = part
            if d:
                target = across(0, d) if h else across(d, 0)
                send(t1.at[pl.ds(h * 16 + p * 4, 4)], r1.at[h, first[h]], 3, p1_r.at[h], target)

    all_sent(hb.at[0], 0)
    all_sent(mo, 1)
    all_sent(blocks(7), 2)
    arrived(gx.at[pl.ds(0, 3)], gx_r.at[0])
    gz[z] = gx[0] + gx[1] + gx[2] + gx[3]
    for d in (4, 3, 5, 2, 6, 1, 7):
        send(gz.at[z], gz.at[z], 5, gz_r.at[0], along_z(d))

    for h in range(2):
        arrived(blocks(12), p1_r.at[h])
        for q in range(4):
            t2[h * 4 + q] = r1[h, 0, q] + r1[h, 1, q] + r1[h, 2, q] + r1[h, 3, q]
        for d in (2, 1, 3):
            q = (second[h] + d) % 4
            target = across(d, 0) if h else across(0, d)
            send(t2.at[h * 4 + q], r2.at[h * 4 + second[h]], 10, p2_r.at[h], target)
        r2[h * 4 + second[h]] = t2[h * 4 + second[h]]
    for h in range(2):
        arrived(blocks(3), p2_r.at[h])
        zb[h, z] = r2[h * 4] + r2[h * 4 + 1] + r2[h * 4 + 2] + r2[h * 4 + 3]
        for d in (4, 3, 5, 2, 6, 1, 7):
            send(zb.at[h, z], zb.at[h, z], 7, z_r.at[h], along_z(d))
    arrived(hs.at[pl.ds(0, 3)], hs_r.at[0])
    kept = hs[0] + hs[1] + hs[2] + hs[3]

    all_sent(blocks(24), 3)
    all_sent(blocks(6), 10)
    all_sent(gx.at[pl.ds(0, 3)], 4)
    all_sent(gz.at[pl.ds(0, 7)], 5)
    arrived(gz.at[pl.ds(0, 7)], gz_r.at[0])
    packed = gz[0]
    for i in range(1, NZ):
        packed = packed + gz[i]
    gram = jnp.concatenate([packed] + [pltpu.roll(packed, 128 - RANK * b, 1) for b in range(1, 4)], axis=0)
    inverse = inverse_factor(gram)[:, :RANK]

    me = slot(0, 0)
    for h in range(2):
        arrived(blocks(7), z_r.at[h])
        value = zb[h, 0]
        for i in range(1, NZ):
            value = value + zb[h, i]
        nb[c, h, me] = full_dot(inverse, value, ((1,), (0,))) / kept[:1]
        mine = nb.at[c, h, me]
        for dx, dy in plane[:-1]:
            send(mine, mine, 8, a_r.at[h, me], across(dx, dy))
        send(mine, mine, 9, ac_r.at[0], partner)
    ortho[...] = full_dot(inverse, left, ((1,), (0,)))
    all_sent(hs.at[pl.ds(0, 3)], 6)
    all_sent(blocks(14), 7)
    for h in range(2):
        for dx, dy in WAITS:
            source = slot(dx, dy)
            theirs = nb.at[c, h, source]
            arrived(theirs, a_r.at[h, source])
            send(theirs, theirs, 9, ac_r.at[0], partner)
    all_sent(blocks(30), 8)
    arrived(nb.at[1 - c], ac_r.at[0])
    all_sent(blocks(32), 9)


def apply_kernel(overflow, ge, nb, ortho, update_hbm, error_hbm, basis_hbm, update, new_error, basis, sem):
    health = 1.0 - overflow[0].astype(F32)
    o1, o2, _ = pieces(ortho[...])
    ortho_pieces = jnp.concatenate([o1, o1, o2], axis=0)
    copies = []
    for k in range(D // WIDTH):
        cols = pl.ds(k * WIDTH, WIDTH)
        count = WIDTH // 128
        new_basis = jnp.concatenate([nb[b // 32, b // 16 % 2, b % 16] for b in range(k * count, (k + 1) * count)], axis=1)
        basis[:, cols] = new_basis
        n1, n2, _ = pieces(new_basis)
        approx = lax.dot_general(
            ortho_pieces,
            jnp.concatenate([n1, n2, n1], axis=0),
            (((0,), (0,)), ((), ())),
            preferred_element_type=F32,
        )
        update[:, cols] = approx.astype(BF16)
        error_value = ge[ROWS:, cols].astype(F32)
        corrected = ge[:ROWS, cols].astype(F32) + error_value
        new_error[:, cols] = jnp.where(health > 0.5, corrected - approx, error_value).astype(BF16)
        for i, (value, out) in enumerate(((basis, basis_hbm), (update, update_hbm), (new_error, error_hbm))):
            copy = pltpu.make_async_copy(value.at[:, cols], out.at[:, cols], sem.at[i, k])
            copy.start()
            copies.append(copy)
    for copy in copies:
        copy.wait()


def on_device(grad_out, error_out, basis_out, overflow):
    grad, error = grad_out[0], error_out[0]
    hbm = pl.BlockSpec(memory_space=pltpu.MemorySpace.HBM)
    smem, whole = pl.BlockSpec(memory_space=pltpu.SMEM), pl.BlockSpec(memory_space=pltpu.VMEM)
    dma = pltpu.SemaphoreType.DMA
    vmem = lambda *shape: pltpu.VMEM(shape, F32)
    block = (RANK, 128)
    operands = [pltpu.with_memory_space_constraint(a, pltpu.HBM) for a in (grad, error, basis_out.T)]
    nb, ortho, ge = pl.pallas_call(
        reduce_kernel,
        out_shape=[
            vmem(2, 2, 16, *block),
            vmem(RANK, ROWS),
            pltpu.VMEM((2 * ROWS, D), BF16),
        ],
        in_specs=[hbm, hbm, hbm, smem],
        out_specs=[whole, whole, whole],
        scratch_shapes=[
            vmem(RANK, D),
            vmem(2, 8, 128),
            vmem(NY, 8, 128),
            vmem(ROWS, HALF),
            vmem(ROWS, HALF),
            pltpu.VMEM((2 * ROWS, HALF), BF16),
            vmem(8, *block),
            vmem(NX, 8, 128),
            vmem(NZ, 8, 128),
            vmem(32, *block),
            vmem(2, 4, 4, *block),
            vmem(8, *block),
            vmem(8, *block),
            vmem(2, NZ, *block),
            dma((3, 2)),
            dma((MPARTS + 1,)),
            dma((1,)),
            dma((1,)),
            dma((1,)),
            dma((1,)),
            dma((2,)),
            dma((2,)),
            dma((2,)),
            dma((2, 16)),
            dma((1,)),
            dma((11,)),
        ],
        compiler_params=pltpu.CompilerParams(collective_id=0, has_side_effects=True, vmem_limit_bytes=32 << 20),
        name="reduce",
    )(*operands, overflow)

    update, new_error, new_basis = pl.pallas_call(
        apply_kernel,
        out_shape=[
            jax.ShapeDtypeStruct((ROWS, D), BF16),
            jax.ShapeDtypeStruct((ROWS, D), BF16),
            jax.ShapeDtypeStruct((RANK, D), F32),
        ],
        in_specs=[smem, whole, whole, whole],
        out_specs=[hbm, hbm, hbm],
        scratch_shapes=[
            pltpu.VMEM((ROWS, D), BF16), pltpu.VMEM((ROWS, D), BF16), vmem(RANK, D), dma((3, D // WIDTH))
        ],
        compiler_params=pltpu.CompilerParams(vmem_limit_bytes=24 << 20),
        name="apply",
    )(overflow, ge, nb, ortho)
    return update, new_error[None], new_basis.T


def solution(mesh):
    return jax.shard_map(
        on_device,
        mesh=mesh,
        in_specs=(P("rep", "shard", None), P("rep", "shard", None), P(), P("rep")),
        out_specs=(P("shard", None), P("rep", "shard", None), P()),
        check_vma=False,
    )
```

```python
import functools

import jax
import jax.numpy as jnp
from jax import lax
from jax.experimental import pallas as pl
from jax.experimental.pallas import tpu as pltpu
from jax.sharding import PartitionSpec as P

MESH = pl.DeviceIdType.MESH
F32, BF16 = jnp.float32, jnp.bfloat16
D, RANK, ROWS = 8192, 32, 128
HALF, QUARTER, MPARTS = D // 2, D // 4, 4
NY, NX, NZ = 4, 4, 8
WIDTH = 1024
WAITS = sorted(((i, j) for i in range(4) for j in range(4) if i or j), key=lambda d: (min(d[0], 4 - d[0]) + min(d[1], 4 - d[1]), d))


def pieces(value):
    first = value.astype(BF16)
    rest = value - first.astype(F32)
    second = rest.astype(BF16)
    third = (rest - second.astype(F32)).astype(BF16)
    return first, second, third


def full_dot(a, b, dims):
    return lax.dot_general(a, b, (dims, ((), ())), precision=lax.Precision.HIGHEST, preferred_element_type=F32)


def inverse_factor(gram):
    row = lax.broadcasted_iota(jnp.int32, (RANK, 128), 0)
    lane = lax.broadcasted_iota(jnp.int32, (RANK, 128), 1)
    diagonal = row == lane
    trace = jnp.sum(jnp.where(diagonal, gram, 0.0), axis=(0, 1), keepdims=True)
    shift = 1e-05 * (trace / RANK)
    work = jnp.where(lane < RANK, gram, 0.0) + jnp.where(diagonal, shift, 0.0)
    work = work + jnp.where(lane - RANK == row, 1.0, 0.0)
    for j in range(RANK - 1):
        column = jnp.broadcast_to(work[:, j : j + 1], (RANK, 128))
        scaled = work[j : j + 1, :] / column[j : j + 1, :]
        work = work - jnp.where(row > j, column, 0.0) * scaled
    pivots = jnp.sum(jnp.where(diagonal, work, 0.0), axis=1, keepdims=True)
    inverse = work * lax.rsqrt(pivots)
    return pltpu.roll(inverse, 128 - RANK, 1)


def reduce_kernel(
    grad_hbm, error_hbm, basis_hbm, overflow, nb, ortho, ge, update, new_error, new_basis,
    bt, hb, hs, mo, mi, mc, ly, gx, gz, t1, r1, t2, r2, zb,
    in_sem, m_r, ly_r, hs_r, gx_r, gz_r, p1_r, p2_r, z_r, a_r, ac_r, s_sem,
):
    rep, shard = lax.axis_index("rep"), lax.axis_index("shard")
    y, c = rep // 2, rep % 2
    x, z = shard // NZ, shard % NZ

    def at(y_, c_, x_, z_):
        return (y_ * 2 + c_, x_ * NZ + z_)

    partner = at(y, 1 - c, x, z)

    def across(dx, dy):
        return at((y + dy) % NY, c, (x + dx) % NX, z)

    def slot(dx, dy):
        return (x + dx) % NX * NY + (y + dy) % NY

    def along_z(d):
        return at(y, c, x, (z + d) % NZ)

    def remote(src, dst, send, recv, device):
        return pltpu.make_async_remote_copy(
            src_ref=src, dst_ref=dst, send_sem=send, recv_sem=recv, device_id=device, device_id_type=MESH
        )

    def send(src, dst, phase, recv_sem, device):
        remote(src, dst, s_sem.at[phase], recv_sem, device).start()

    def arrived(like, recv_sem):
        remote(like, like, s_sem.at[0], recv_sem, partner).wait_recv()

    def all_sent(like, phase):
        remote(like, like, s_sem.at[phase], m_r.at[0], partner).wait_send()

    def blocks(count):
        return t1.at[pl.ds(0, count)]

    halves = [(1 - c) * HALF, c * HALF]
    loads = []
    for i, start in enumerate(halves):
        cols = pl.ds(pl.multiple_of(start, HALF), HALF)
        group = [
            pltpu.make_async_copy(grad_hbm.at[:, cols], ge.at[pl.ds(0, ROWS), cols], in_sem.at[0, i]),
            pltpu.make_async_copy(error_hbm.at[:, cols], ge.at[pl.ds(ROWS, ROWS), cols], in_sem.at[1, i]),
            pltpu.make_async_copy(basis_hbm.at[:, cols], bt.at[:, cols], in_sem.at[2, i]),
        ]
        for copy in group:
            copy.start()
        loads.append(group)

    barrier = pltpu.get_barrier_semaphore()
    replicas = [(2, 0), (2, 1), (1, 0), (3, 0), (1, 1), (3, 1), (0, 1)]
    replicas = [at((y + dy) % NY, (c + dc) % 2, x, z) for dy, dc in replicas]
    plane = [(dx, dy) for dx in (2, 1, 3, 0) for dy in (2, 1, 3, 0)]
    others = replicas + [across(dx, dy) for dx, dy in plane if dx] + [along_z(d) for d in range(1, NZ)]
    for other in others:
        pl.semaphore_signal(barrier, inc=1, device_id=other, device_id_type=MESH)

    health = jnp.full((8, 128), 1.0 - overflow[0].astype(F32), F32)
    hb[0] = health
    weight = health[:1, :1]

    def corrected(start):
        cols = pl.ds(pl.multiple_of(start, 512), 512)
        return (ge[:ROWS, cols].astype(F32) + ge[ROWS:, cols].astype(F32)) * weight

    def project(start):
        cols = pl.ds(pl.multiple_of(start, 512), 1024)
        basis = jnp.concatenate(pieces(bt[:, cols]), axis=0)
        return lax.dot_general(basis, ge[:, cols], (((1,), (1,)), ((), ())), preferred_element_type=F32)

    for copy in loads[0]:
        copy.wait()
    acc = jnp.zeros((3 * RANK, 2 * ROWS), F32)
    for k in range(HALF // 1024):
        acc += project(halves[0] + k * 1024)
        for i in range(2):
            mo[:, pl.ds(k * 1024 + i * 512, 512)] = corrected(halves[0] + k * 1024 + i * 512)
    pl.semaphore_wait(barrier, len(others))
    send(hb.at[0], hb.at[1], 0, m_r.at[MPARTS], partner)
    for k in range(MPARTS):
        rows = pl.ds(k * (ROWS // MPARTS), ROWS // MPARTS)
        send(mo.at[rows], mi.at[rows], 1, m_r.at[k], partner)
    for copy in loads[1]:
        copy.wait()
    for k in range(HALF // 1024):
        acc += project(halves[1] + k * 1024)
    both = acc[:RANK] + acc[RANK : 2 * RANK] + acc[2 * RANK :]

    ly[rep] = (both[:, :ROWS] + both[:, ROWS:]) * weight
    for other in replicas:
        send(ly.at[rep], ly.at[rep], 2, ly_r.at[0], other)

    for k in range(MPARTS):
        size = ROWS // MPARTS
        rows = pl.ds(k * size, size)
        arrived(mi.at[rows], m_r.at[k])
        for i in range(HALF // 1024):
            own = pl.ds(pl.multiple_of(halves[1] + i * 1024, 1024), 1024)
            cols = pl.ds(i * 1024, 1024)
            value = ge[rows, own].astype(F32) + ge[pl.ds(ROWS + k * size, size), own].astype(F32)
            value = value * weight + mi[rows, cols]
            high = value.astype(BF16)
            mc[rows, cols] = high
            mc[pl.ds(ROWS + k * size, size), cols] = (value - high.astype(F32)).astype(BF16)
    arrived(hb.at[1], m_r.at[MPARTS])
    hs[y] = hb[0] + hb[1]
    for d in (2, 1, 3):
        send(hs.at[y], hs.at[y], 6, hs_r.at[0], across(0, d))

    arrived(ly.at[pl.ds(0, 7)], ly_r.at[0])
    left = ly[0]
    for i in range(1, 8):
        left = left + ly[i]

    gram = full_dot(left, jnp.concatenate([left] * 4, axis=0), ((1,), (1,)))
    lane_group = lax.broadcasted_iota(jnp.int32, (8, 128), 1) // RANK
    packed = gram[:8]
    for b in range(1, 4):
        packed = jnp.where(lane_group == b, gram[8 * b : 8 * b + 8], packed)
    gx[x] = packed
    for d in (2, 1, 3):
        send(gx.at[x], gx.at[x], 4, gx_r.at[0], across(d, 0))
    weighted = jnp.concatenate(pieces(left), axis=0)
    weighted = jnp.concatenate([weighted, weighted], axis=1)
    first = (x, y)
    second = (y, x)
    for d in (2, 1, 3, 0):
        for h in range(2):
            p = (first[h] + d) % 4
            group = [h * 16 + (p * 4 + q, q * 4 + p)[h] for q in range(4)]
            if h:
                rows = jnp.concatenate([mc[:, pl.ds(pl.multiple_of(b * 128, 128), 128)] for b in group], axis=1)
            else:
                rows = mc[:, pl.ds(pl.multiple_of(group[0] * 128, 512), 512)]
            out = lax.dot_general(weighted, rows, (((1,), (0,)), ((), ())), preferred_element_type=F32)
            value = out[:RANK] + out[RANK : 2 * RANK] + out[2 * RANK :]
            for q in range(4):
                part = value[:, q * 128 : (q + 1) * 128]
                if d == 0:
                    r1[h, p, q] = part
                else:
                    t1[h * 16 + p * 4 + q] = part
            if d:
                target = across(0, d) if h else across(d, 0)
                send(t1.at[pl.ds(h * 16 + p * 4, 4)], r1.at[h, first[h]], 3, p1_r.at[h], target)

    all_sent(hb.at[0], 0)
    all_sent(mo, 1)
    all_sent(blocks(7), 2)
    arrived(gx.at[pl.ds(0, 3)], gx_r.at[0])
    gz[z] = gx[0] + gx[1] + gx[2] + gx[3]
    for d in (4, 3, 5, 2, 6, 1, 7):
        send(gz.at[z], gz.at[z], 5, gz_r.at[0], along_z(d))

    for h in range(2):
        arrived(blocks(12), p1_r.at[h])
        for q in range(4):
            t2[h * 4 + q] = r1[h, 0, q] + r1[h, 1, q] + r1[h, 2, q] + r1[h, 3, q]
        for d in (2, 1, 3):
            q = (second[h] + d) % 4
            target = across(d, 0) if h else across(0, d)
            send(t2.at[h * 4 + q], r2.at[h * 4 + second[h]], 10, p2_r.at[h], target)
        r2[h * 4 + second[h]] = t2[h * 4 + second[h]]
    for h in range(2):
        arrived(blocks(3), p2_r.at[h])
        zb[h, z] = r2[h * 4] + r2[h * 4 + 1] + r2[h * 4 + 2] + r2[h * 4 + 3]
        for d in (1, 7, 2, 6, 3, 5, 4):
            send(zb.at[h, z], zb.at[h, z], 7, z_r.at[h], along_z(d))
    arrived(hs.at[pl.ds(0, 3)], hs_r.at[0])
    kept = hs[0] + hs[1] + hs[2] + hs[3]

    all_sent(blocks(24), 3)
    all_sent(blocks(6), 10)
    all_sent(gx.at[pl.ds(0, 3)], 4)
    all_sent(gz.at[pl.ds(0, 7)], 5)
    arrived(gz.at[pl.ds(0, 7)], gz_r.at[0])
    packed = gz[0]
    for i in range(1, NZ):
        packed = packed + gz[i]
    gram = jnp.concatenate([packed] + [pltpu.roll(packed, 128 - RANK * b, 1) for b in range(1, 4)], axis=0)
    inverse = inverse_factor(gram)[:, :RANK]

    me = slot(0, 0)
    for h in range(2):
        arrived(blocks(7), z_r.at[h])
        value = zb[h, 0]
        for i in range(1, NZ):
            value = value + zb[h, i]
        nb[c, h, me] = full_dot(inverse, value, ((1,), (0,))) / kept[:1]
        mine = nb.at[c, h, me]
        for dx, dy in plane[:-1]:
            send(mine, mine, 8, a_r.at[h, me], across(dx, dy))
        send(mine, mine, 9, ac_r.at[h], partner)
    ortho[...] = full_dot(inverse, left, ((1,), (0,)))
    all_sent(hs.at[pl.ds(0, 3)], 6)
    all_sent(blocks(14), 7)
    left_pieces = stacked(ortho[...])

    def finish(core, h):
        for k in range(QUARTER // WIDTH):
            cols = pl.ds(pl.multiple_of(core * HALF + h * QUARTER + k * WIDTH, WIDTH), WIDTH)
            values = [nb[core, h, k * (WIDTH // 128) + i] for i in range(WIDTH // 128)]
            apply(health[:1, :1], left_pieces, values, ge, update, new_error, new_basis, cols, cols)

    for h in range(2):
        for dx, dy in WAITS:
            source = slot(dx, dy)
            theirs = nb.at[c, h, source]
            arrived(theirs, a_r.at[h, source])
            send(theirs, theirs, 9, ac_r.at[h], partner)
        finish(c, h)
    all_sent(blocks(30), 8)
    arrived(blocks(16), ac_r.at[0])
    finish(1 - c, 0)
    arrived(blocks(16), ac_r.at[1])
    all_sent(blocks(32), 9)


def stacked(ortho):
    o1, o2, _ = pieces(ortho)
    return jnp.concatenate([o1, o1, o2], axis=0)


def apply(health, ortho_pieces, blocks, ge, update, new_error, basis, cols, to):
    value = jnp.concatenate(blocks, axis=1)
    basis[:, to] = value
    n1, n2, _ = pieces(value)
    approx = lax.dot_general(
        ortho_pieces, jnp.concatenate([n1, n2, n1], axis=0), (((0,), (0,)), ((), ())), preferred_element_type=F32
    )
    update[:, to] = approx.astype(BF16)
    error_value = ge[ROWS:, cols].astype(F32)
    corrected = ge[:ROWS, cols].astype(F32) + error_value
    new_error[:, to] = jnp.where(health > 0.5, corrected - approx, error_value).astype(BF16)


def last_kernel(
    overflow, nb, ortho, ge, update, new_error, basis, update_hbm, error_hbm, basis_hbm, update_s, error_s, basis_s, sem
):
    c = lax.axis_index("rep") % 2
    results = ((update, update_s, update_hbm), (new_error, error_s, error_hbm), (basis, basis_s, basis_hbm))
    copies = []
    for k, start in enumerate((c * HALF, c * HALF + QUARTER, (1 - c) * HALF)):
        cols = pl.ds(pl.multiple_of(start, QUARTER), QUARTER)
        for i, (done, _, out) in enumerate(results):
            copies.append(pltpu.make_async_copy(done.at[:, cols], out.at[:, cols], sem.at[i, k]))
            copies[-1].start()
    health = 1.0 - overflow[0].astype(F32)
    ortho_pieces = stacked(ortho[...])
    for k in range(QUARTER // WIDTH):
        to = pl.ds(k * WIDTH, WIDTH)
        cols = pl.ds(pl.multiple_of((1 - c) * HALF + QUARTER + k * WIDTH, WIDTH), WIDTH)
        values = [nb[1 - c, 1, k * (WIDTH // 128) + i] for i in range(WIDTH // 128)]
        apply(health, ortho_pieces, values, ge, update_s, error_s, basis_s, cols, to)
        for i, (_, new, out) in enumerate(results):
            copies.append(pltpu.make_async_copy(new.at[:, to], out.at[:, cols], sem.at[i, 3 + k]))
            copies[-1].start()
    for copy in copies:
        copy.wait()


def on_device(grad_out, error_out, basis_out, overflow):
    grad, error = grad_out[0], error_out[0]
    hbm = pl.BlockSpec(memory_space=pltpu.MemorySpace.HBM)
    smem, whole = pl.BlockSpec(memory_space=pltpu.SMEM), pl.BlockSpec(memory_space=pltpu.VMEM)
    dma = pltpu.SemaphoreType.DMA
    vmem = lambda *shape: pltpu.VMEM(shape, F32)
    block = (RANK, 128)
    operands = [pltpu.with_memory_space_constraint(a, pltpu.HBM) for a in (grad, error, basis_out.T)]
    outs = pl.pallas_call(
        reduce_kernel,
        out_shape=[
            vmem(2, 2, 16, *block),
            vmem(RANK, ROWS),
            pltpu.VMEM((2 * ROWS, D), BF16),
            pltpu.VMEM((ROWS, D), BF16),
            pltpu.VMEM((ROWS, D), BF16),
            vmem(RANK, D),
        ],
        in_specs=[hbm, hbm, hbm, smem],
        out_specs=[whole] * 6,
        scratch_shapes=[
            vmem(RANK, D),
            vmem(2, 8, 128),
            vmem(NY, 8, 128),
            vmem(ROWS, HALF),
            vmem(ROWS, HALF),
            pltpu.VMEM((2 * ROWS, HALF), BF16),
            vmem(8, *block),
            vmem(NX, 8, 128),
            vmem(NZ, 8, 128),
            vmem(32, *block),
            vmem(2, 4, 4, *block),
            vmem(8, *block),
            vmem(8, *block),
            vmem(2, NZ, *block),
            dma((3, 2)),
            dma((MPARTS + 1,)),
            dma((1,)),
            dma((1,)),
            dma((1,)),
            dma((1,)),
            dma((2,)),
            dma((2,)),
            dma((2,)),
            dma((2, 16)),
            dma((2,)),
            dma((11,)),
        ],
        compiler_params=pltpu.CompilerParams(collective_id=0, has_side_effects=True, vmem_limit_bytes=32 << 20),
        name="reduce",
    )(*operands, overflow)

    update, new_error, new_basis = pl.pallas_call(
        last_kernel,
        out_shape=[
            jax.ShapeDtypeStruct((ROWS, D), BF16),
            jax.ShapeDtypeStruct((ROWS, D), BF16),
            jax.ShapeDtypeStruct((RANK, D), F32),
        ],
        in_specs=[smem] + [whole] * 6,
        out_specs=[hbm, hbm, hbm],
        scratch_shapes=[
            pltpu.VMEM((ROWS, QUARTER), BF16), pltpu.VMEM((ROWS, QUARTER), BF16), vmem(RANK, QUARTER), dma((3, 3 + QUARTER // WIDTH))
        ],
        compiler_params=pltpu.CompilerParams(vmem_limit_bytes=16 << 20),
        name="last",
    )(overflow, *outs)
    return update, new_error[None], new_basis.T


def solution(mesh):
    return jax.shard_map(
        on_device,
        mesh=mesh,
        in_specs=(P("rep", "shard", None), P("rep", "shard", None), P(), P("rep")),
        out_specs=(P("shard", None), P("rep", "shard", None), P()),
        check_vma=False,
    )
```

```python
import functools

import jax
import jax.numpy as jnp
from jax import lax
from jax.experimental import pallas as pl
from jax.experimental.pallas import tpu as pltpu
from jax.sharding import PartitionSpec as P

MESH = pl.DeviceIdType.MESH
F32, BF16 = jnp.float32, jnp.bfloat16
D, RANK, ROWS = 8192, 32, 128
HALF, QUARTER, MPARTS = D // 2, D // 4, 2
NY, NX, NZ = 4, 4, 8
WIDTH = 1024
WAITS = sorted(((i, j) for i in range(4) for j in range(4) if i or j), key=lambda d: (min(d[0], 4 - d[0]) + min(d[1], 4 - d[1]), d))


def pieces(value):
    first = value.astype(BF16)
    rest = value - first.astype(F32)
    second = rest.astype(BF16)
    third = (rest - second.astype(F32)).astype(BF16)
    return first, second, third


def full_dot(a, b, dims):
    return lax.dot_general(a, b, (dims, ((), ())), precision=lax.Precision.HIGHEST, preferred_element_type=F32)


def inverse_factor(gram):
    row = lax.broadcasted_iota(jnp.int32, (RANK, 128), 0)
    lane = lax.broadcasted_iota(jnp.int32, (RANK, 128), 1)
    diagonal = row == lane
    trace = jnp.sum(jnp.where(diagonal, gram, 0.0), axis=(0, 1), keepdims=True)
    shift = 1e-05 * (trace / RANK)
    work = jnp.where(lane < RANK, gram, 0.0) + jnp.where(diagonal, shift, 0.0)
    work = work + jnp.where(lane - RANK == row, 1.0, 0.0)
    for j in range(RANK - 1):
        column = jnp.broadcast_to(work[:, j : j + 1], (RANK, 128))
        scaled = work[j : j + 1, :] / column[j : j + 1, :]
        work = work - jnp.where(row > j, column, 0.0) * scaled
    pivots = jnp.sum(jnp.where(diagonal, work, 0.0), axis=1, keepdims=True)
    inverse = work * lax.rsqrt(pivots)
    return pltpu.roll(inverse, 128 - RANK, 1)


def reduce_kernel(
    grad_hbm, error_hbm, basis_hbm, overflow, nb, ortho, ge, update, new_error, new_basis,
    bt, hb, hs, mo, mi, mc, ly, gx, gz, t1, r1, t2, r2, zb,
    in_sem, m_r, ly_r, hs_r, gx_r, gz_r, p1_r, p2_r, z_r, a_r, ac_r, s_sem,
):
    rep, shard = lax.axis_index("rep"), lax.axis_index("shard")
    y, c = rep // 2, rep % 2
    x, z = shard // NZ, shard % NZ

    def at(y_, c_, x_, z_):
        return (y_ * 2 + c_, x_ * NZ + z_)

    partner = at(y, 1 - c, x, z)

    def across(dx, dy):
        return at((y + dy) % NY, c, (x + dx) % NX, z)

    def slot(dx, dy):
        return (x + dx) % NX * NY + (y + dy) % NY

    def along_z(d):
        return at(y, c, x, (z + d) % NZ)

    def remote(src, dst, send, recv, device):
        return pltpu.make_async_remote_copy(
            src_ref=src, dst_ref=dst, send_sem=send, recv_sem=recv, device_id=device, device_id_type=MESH
        )

    def send(src, dst, phase, recv_sem, device):
        remote(src, dst, s_sem.at[phase], recv_sem, device).start()

    def arrived(like, recv_sem):
        remote(like, like, s_sem.at[0], recv_sem, partner).wait_recv()

    def all_sent(like, phase):
        remote(like, like, s_sem.at[phase], m_r.at[0], partner).wait_send()

    def blocks(count):
        return t1.at[pl.ds(0, count)]

    halves = [(1 - c) * HALF, c * HALF]
    loads = []
    for i, start in enumerate(halves):
        cols = pl.ds(pl.multiple_of(start, HALF), HALF)
        group = [
            pltpu.make_async_copy(grad_hbm.at[:, cols], ge.at[pl.ds(0, ROWS), cols], in_sem.at[0, i]),
            pltpu.make_async_copy(error_hbm.at[:, cols], ge.at[pl.ds(ROWS, ROWS), cols], in_sem.at[1, i]),
            pltpu.make_async_copy(basis_hbm.at[:, cols], bt.at[:, cols], in_sem.at[2, i]),
        ]
        for copy in group:
            copy.start()
        loads.append(group)

    barrier = pltpu.get_barrier_semaphore()
    replicas = [(2, 1), (1, 1), (3, 1), (2, 0), (1, 0), (3, 0), (0, 1)]
    replicas = [at((y + dy) % NY, (c + dc) % 2, x, z) for dy, dc in replicas]
    plane = [(dx, dy) for dx in (2, 1, 3, 0) for dy in (2, 1, 3, 0)]
    others = replicas + [across(dx, dy) for dx, dy in plane if dx] + [along_z(d) for d in range(1, NZ)]
    for other in others:
        pl.semaphore_signal(barrier, inc=1, device_id=other, device_id_type=MESH)

    health = jnp.full((8, 128), 1.0 - overflow[0].astype(F32), F32)
    hb[0] = health
    weight = health[:1, :1]

    def corrected(start):
        cols = pl.ds(pl.multiple_of(start, 512), 512)
        return (ge[:ROWS, cols].astype(F32) + ge[ROWS:, cols].astype(F32)) * weight

    def project(start):
        cols = pl.ds(pl.multiple_of(start, 512), 1024)
        basis = jnp.concatenate(pieces(bt[:, cols]), axis=0)
        return lax.dot_general(basis, ge[:, cols], (((1,), (1,)), ((), ())), preferred_element_type=F32)

    for copy in loads[0]:
        copy.wait()
    acc = jnp.zeros((3 * RANK, 2 * ROWS), F32)
    for k in range(HALF // 1024):
        acc += project(halves[0] + k * 1024)
        for i in range(2):
            mo[:, pl.ds(k * 1024 + i * 512, 512)] = corrected(halves[0] + k * 1024 + i * 512)
    pl.semaphore_wait(barrier, len(others))
    send(hb.at[0], hb.at[1], 0, m_r.at[MPARTS], partner)
    for k in range(MPARTS):
        rows = pl.ds(k * (ROWS // MPARTS), ROWS // MPARTS)
        send(mo.at[rows], mi.at[rows], 1, m_r.at[k], partner)
    for copy in loads[1]:
        copy.wait()
    for k in range(HALF // 1024):
        acc += project(halves[1] + k * 1024)
    both = acc[:RANK] + acc[RANK : 2 * RANK] + acc[2 * RANK :]

    ly[rep] = (both[:, :ROWS] + both[:, ROWS:]) * weight
    for other in replicas:
        send(ly.at[rep], ly.at[rep], 2, ly_r.at[0], other)

    for k in range(MPARTS):
        size = ROWS // MPARTS
        rows = pl.ds(k * size, size)
        arrived(mi.at[rows], m_r.at[k])
        for i in range(HALF // 1024):
            own = pl.ds(pl.multiple_of(halves[1] + i * 1024, 1024), 1024)
            cols = pl.ds(i * 1024, 1024)
            value = ge[rows, own].astype(F32) + ge[pl.ds(ROWS + k * size, size), own].astype(F32)
            value = value * weight + mi[rows, cols]
            high = value.astype(BF16)
            mc[rows, cols] = high
            mc[pl.ds(ROWS + k * size, size), cols] = (value - high.astype(F32)).astype(BF16)
    arrived(hb.at[1], m_r.at[MPARTS])
    hs[y] = hb[0] + hb[1]
    for d in (2, 1, 3):
        send(hs.at[y], hs.at[y], 6, hs_r.at[0], across(0, d))

    arrived(ly.at[pl.ds(0, 7)], ly_r.at[0])
    left = ly[0]
    for i in range(1, 8):
        left = left + ly[i]

    gram = full_dot(left, jnp.concatenate([left] * 4, axis=0), ((1,), (1,)))
    lane_group = lax.broadcasted_iota(jnp.int32, (8, 128), 1) // RANK
    packed = gram[:8]
    for b in range(1, 4):
        packed = jnp.where(lane_group == b, gram[8 * b : 8 * b + 8], packed)
    gx[x] = packed
    for d in (2, 1, 3):
        send(gx.at[x], gx.at[x], 4, gx_r.at[0], across(d, 0))
    weighted = jnp.concatenate(pieces(left), axis=0)
    weighted = jnp.concatenate([weighted, weighted], axis=1)
    first = (x, y)
    second = (y, x)
    for d in (2, 1, 3, 0):
        for h in range(2):
            p = (first[h] + d) % 4
            group = [h * 16 + (p * 4 + q, q * 4 + p)[h] for q in range(4)]
            if h:
                rows = jnp.concatenate([mc[:, pl.ds(pl.multiple_of(b * 128, 128), 128)] for b in group], axis=1)
            else:
                rows = mc[:, pl.ds(pl.multiple_of(group[0] * 128, 512), 512)]
            out = lax.dot_general(weighted, rows, (((1,), (0,)), ((), ())), preferred_element_type=F32)
            value = out[:RANK] + out[RANK : 2 * RANK] + out[2 * RANK :]
            for q in range(4):
                part = value[:, q * 128 : (q + 1) * 128]
                if d == 0:
                    r1[h, p, q] = part
                else:
                    t1[h * 16 + p * 4 + q] = part
            if d:
                target = across(0, d) if h else across(d, 0)
                send(t1.at[pl.ds(h * 16 + p * 4, 4)], r1.at[h, first[h]], 3, p1_r.at[h], target)

    all_sent(hb.at[0], 0)
    all_sent(mo, 1)
    all_sent(blocks(7), 2)
    arrived(gx.at[pl.ds(0, 3)], gx_r.at[0])
    gz[z] = gx[0] + gx[1] + gx[2] + gx[3]
    for d in (4, 3, 5, 2, 6, 1, 7):
        send(gz.at[z], gz.at[z], 5, gz_r.at[0], along_z(d))

    for h in range(2):
        arrived(blocks(12), p1_r.at[h])
        for q in range(4):
            t2[h * 4 + q] = r1[h, 0, q] + r1[h, 1, q] + r1[h, 2, q] + r1[h, 3, q]
        for d in (2, 1, 3):
            q = (second[h] + d) % 4
            target = across(d, 0) if h else across(0, d)
            send(t2.at[h * 4 + q], r2.at[h * 4 + second[h]], 10, p2_r.at[h], target)
        r2[h * 4 + second[h]] = t2[h * 4 + second[h]]
    for h in range(2):
        arrived(blocks(3), p2_r.at[h])
        zb[h, z] = r2[h * 4] + r2[h * 4 + 1] + r2[h * 4 + 2] + r2[h * 4 + 3]
        for d in (4, 3, 5, 2, 6, 1, 7):
            send(zb.at[h, z], zb.at[h, z], 7, z_r.at[h], along_z(d))
    arrived(hs.at[pl.ds(0, 3)], hs_r.at[0])
    kept = hs[0] + hs[1] + hs[2] + hs[3]

    all_sent(blocks(24), 3)
    all_sent(blocks(6), 10)
    all_sent(gx.at[pl.ds(0, 3)], 4)
    all_sent(gz.at[pl.ds(0, 7)], 5)
    arrived(gz.at[pl.ds(0, 7)], gz_r.at[0])
    packed = gz[0]
    for i in range(1, NZ):
        packed = packed + gz[i]
    gram = jnp.concatenate([packed] + [pltpu.roll(packed, 128 - RANK * b, 1) for b in range(1, 4)], axis=0)
    inverse = inverse_factor(gram)[:, :RANK]

    me = slot(0, 0)
    for h in range(2):
        arrived(blocks(7), z_r.at[h])
        value = zb[h, 0]
        for i in range(1, NZ):
            value = value + zb[h, i]
        nb[c, h, me] = full_dot(inverse, value, ((1,), (0,))) / kept[:1]
        mine = nb.at[c, h, me]
        for dx, dy in plane[:-1]:
            send(mine, mine, 8, a_r.at[h, me], across(dx, dy))
        send(mine, mine, 9, ac_r.at[h], partner)
    ortho[...] = full_dot(inverse, left, ((1,), (0,)))
    all_sent(hs.at[pl.ds(0, 3)], 6)
    all_sent(blocks(14), 7)
    left_pieces = stacked(ortho[...])

    def finish(core, h):
        for k in range(QUARTER // WIDTH):
            cols = pl.ds(pl.multiple_of(core * HALF + h * QUARTER + k * WIDTH, WIDTH), WIDTH)
            values = [nb[core, h, k * (WIDTH // 128) + i] for i in range(WIDTH // 128)]
            apply(health[:1, :1], left_pieces, values, ge, update, new_error, new_basis, cols, cols)

    for h in range(2):
        for dx, dy in WAITS:
            source = slot(dx, dy)
            theirs = nb.at[c, h, source]
            arrived(theirs, a_r.at[h, source])
            send(theirs, theirs, 9, ac_r.at[h], partner)
        finish(c, h)
    all_sent(blocks(30), 8)
    arrived(blocks(16), ac_r.at[0])
    finish(1 - c, 0)
    arrived(blocks(16), ac_r.at[1])
    all_sent(blocks(32), 9)


def stacked(ortho):
    o1, o2, _ = pieces(ortho)
    return jnp.concatenate([o1, o1, o2], axis=0)


def apply(health, ortho_pieces, blocks, ge, update, new_error, basis, cols, to):
    value = jnp.concatenate(blocks, axis=1)
    basis[:, to] = value
    n1, n2, _ = pieces(value)
    approx = lax.dot_general(
        ortho_pieces, jnp.concatenate([n1, n2, n1], axis=0), (((0,), (0,)), ((), ())), preferred_element_type=F32
    )
    update[:, to] = approx.astype(BF16)
    error_value = ge[ROWS:, cols].astype(F32)
    corrected = ge[:ROWS, cols].astype(F32) + error_value
    new_error[:, to] = jnp.where(health > 0.5, corrected - approx, error_value).astype(BF16)


def last_kernel(
    overflow, nb, ortho, ge, update, new_error, basis, update_hbm, error_hbm, basis_hbm, update_s, error_s, basis_s, sem
):
    c = lax.axis_index("rep") % 2
    results = ((update, update_s, update_hbm), (new_error, error_s, error_hbm), (basis, basis_s, basis_hbm))
    copies = []
    for k, start in enumerate((c * HALF, c * HALF + QUARTER, (1 - c) * HALF)):
        cols = pl.ds(pl.multiple_of(start, QUARTER), QUARTER)
        for i, (done, _, out) in enumerate(results):
            copies.append(pltpu.make_async_copy(done.at[:, cols], out.at[:, cols], sem.at[i, k]))
            copies[-1].start()
    health = 1.0 - overflow[0].astype(F32)
    ortho_pieces = stacked(ortho[...])
    for k in range(QUARTER // WIDTH):
        to = pl.ds(k * WIDTH, WIDTH)
        cols = pl.ds(pl.multiple_of((1 - c) * HALF + QUARTER + k * WIDTH, WIDTH), WIDTH)
        values = [nb[1 - c, 1, k * (WIDTH // 128) + i] for i in range(WIDTH // 128)]
        apply(health, ortho_pieces, values, ge, update_s, error_s, basis_s, cols, to)
        for i, (_, new, out) in enumerate(results):
            copies.append(pltpu.make_async_copy(new.at[:, to], out.at[:, cols], sem.at[i, 3 + k]))
            copies[-1].start()
    for copy in copies:
        copy.wait()


def on_device(grad_out, error_out, basis_out, overflow):
    grad, error = grad_out[0], error_out[0]
    hbm = pl.BlockSpec(memory_space=pltpu.MemorySpace.HBM)
    smem, whole = pl.BlockSpec(memory_space=pltpu.SMEM), pl.BlockSpec(memory_space=pltpu.VMEM)
    dma = pltpu.SemaphoreType.DMA
    vmem = lambda *shape: pltpu.VMEM(shape, F32)
    block = (RANK, 128)
    operands = [pltpu.with_memory_space_constraint(a, pltpu.HBM) for a in (grad, error, basis_out.T)]
    outs = pl.pallas_call(
        reduce_kernel,
        out_shape=[
            vmem(2, 2, 16, *block),
            vmem(RANK, ROWS),
            pltpu.VMEM((2 * ROWS, D), BF16),
            pltpu.VMEM((ROWS, D), BF16),
            pltpu.VMEM((ROWS, D), BF16),
            vmem(RANK, D),
        ],
        in_specs=[hbm, hbm, hbm, smem],
        out_specs=[whole] * 6,
        scratch_shapes=[
            vmem(RANK, D),
            vmem(2, 8, 128),
            vmem(NY, 8, 128),
            vmem(ROWS, HALF),
            vmem(ROWS, HALF),
            pltpu.VMEM((2 * ROWS, HALF), BF16),
            vmem(8, *block),
            vmem(NX, 8, 128),
            vmem(NZ, 8, 128),
            vmem(32, *block),
            vmem(2, 4, 4, *block),
            vmem(8, *block),
            vmem(8, *block),
            vmem(2, NZ, *block),
            dma((3, 2)),
            dma((MPARTS + 1,)),
            dma((1,)),
            dma((1,)),
            dma((1,)),
            dma((1,)),
            dma((2,)),
            dma((2,)),
            dma((2,)),
            dma((2, 16)),
            dma((2,)),
            dma((11,)),
        ],
        compiler_params=pltpu.CompilerParams(collective_id=0, has_side_effects=True, vmem_limit_bytes=32 << 20),
        name="reduce",
    )(*operands, overflow)

    update, new_error, new_basis = pl.pallas_call(
        last_kernel,
        out_shape=[
            jax.ShapeDtypeStruct((ROWS, D), BF16),
            jax.ShapeDtypeStruct((ROWS, D), BF16),
            jax.ShapeDtypeStruct((RANK, D), F32),
        ],
        in_specs=[smem] + [whole] * 6,
        out_specs=[hbm, hbm, hbm],
        scratch_shapes=[
            pltpu.VMEM((ROWS, QUARTER), BF16), pltpu.VMEM((ROWS, QUARTER), BF16), vmem(RANK, QUARTER), dma((3, 3 + QUARTER // WIDTH))
        ],
        compiler_params=pltpu.CompilerParams(vmem_limit_bytes=16 << 20),
        name="last",
    )(overflow, *outs)
    return update, new_error[None], new_basis.T


def solution(mesh):
    return jax.shard_map(
        on_device,
        mesh=mesh,
        in_specs=(P("rep", "shard", None), P("rep", "shard", None), P(), P("rep")),
        out_specs=(P("shard", None), P("rep", "shard", None), P()),
        check_vma=False,
    )
```

```python
import functools

import jax
import jax.numpy as jnp
from jax import lax
from jax.experimental import pallas as pl
from jax.experimental.pallas import tpu as pltpu
from jax.sharding import PartitionSpec as P

MESH = pl.DeviceIdType.MESH
F32, BF16 = jnp.float32, jnp.bfloat16
D, RANK, ROWS = 8192, 32, 128
HALF, QUARTER, MPARTS = D // 2, D // 4, 2
NY, NX, NZ = 4, 4, 8
WIDTH = 1024
WAITS = sorted(((i, j) for i in range(4) for j in range(4) if i or j), key=lambda d: (min(d[0], 4 - d[0]) + min(d[1], 4 - d[1]), d))


def pieces(value):
    first = value.astype(BF16)
    rest = value - first.astype(F32)
    second = rest.astype(BF16)
    third = (rest - second.astype(F32)).astype(BF16)
    return first, second, third


def full_dot(a, b, dims):
    return lax.dot_general(a, b, (dims, ((), ())), precision=lax.Precision.HIGHEST, preferred_element_type=F32)


def inverse_factor(gram):
    row = lax.broadcasted_iota(jnp.int32, (RANK, 128), 0)
    lane = lax.broadcasted_iota(jnp.int32, (RANK, 128), 1)
    diagonal = row == lane
    trace = jnp.sum(jnp.where(diagonal, gram, 0.0), axis=(0, 1), keepdims=True)
    shift = 1e-05 * (trace / RANK)
    work = jnp.where(lane < RANK, gram, 0.0) + jnp.where(diagonal, shift, 0.0)
    work = work + jnp.where(lane - RANK == row, 1.0, 0.0)
    for j in range(RANK - 1):
        column = jnp.broadcast_to(work[:, j : j + 1], (RANK, 128))
        scaled = work[j : j + 1, :] / column[j : j + 1, :]
        work = work - jnp.where(row > j, column, 0.0) * scaled
    pivots = jnp.sum(jnp.where(diagonal, work, 0.0), axis=1, keepdims=True)
    inverse = work * lax.rsqrt(pivots)
    return pltpu.roll(inverse, 128 - RANK, 1)


def reduce_kernel(
    grad_hbm, error_hbm, basis_hbm, overflow, nb, ortho, ge, update, new_error, new_basis,
    bt, hb, hs, mo, mi, mc, ly, gx, gz, t1, r1, t2, r2, zb,
    in_sem, m_r, ly_r, hs_r, gx_r, gz_r, p1_r, p2_r, z_r, a_r, ac_r, s_sem,
):
    rep, shard = lax.axis_index("rep"), lax.axis_index("shard")
    y, c = rep // 2, rep % 2
    x, z = shard // NZ, shard % NZ

    def at(y_, c_, x_, z_):
        return (y_ * 2 + c_, x_ * NZ + z_)

    partner = at(y, 1 - c, x, z)

    def across(dx, dy):
        return at((y + dy) % NY, c, (x + dx) % NX, z)

    def slot(dx, dy):
        return (x + dx) % NX * NY + (y + dy) % NY

    def along_z(d):
        return at(y, c, x, (z + d) % NZ)

    def remote(src, dst, send, recv, device):
        return pltpu.make_async_remote_copy(
            src_ref=src, dst_ref=dst, send_sem=send, recv_sem=recv, device_id=device, device_id_type=MESH
        )

    def send(src, dst, phase, recv_sem, device):
        remote(src, dst, s_sem.at[phase], recv_sem, device).start()

    def arrived(like, recv_sem):
        remote(like, like, s_sem.at[0], recv_sem, partner).wait_recv()

    def all_sent(like, phase):
        remote(like, like, s_sem.at[phase], m_r.at[0], partner).wait_send()

    def blocks(count):
        return t1.at[pl.ds(0, count)]

    halves = [(1 - c) * HALF, c * HALF]
    loads = []
    for i, start in enumerate(halves):
        cols = pl.ds(pl.multiple_of(start, HALF), HALF)
        group = [
            pltpu.make_async_copy(grad_hbm.at[:, cols], ge.at[pl.ds(0, ROWS), cols], in_sem.at[0, i]),
            pltpu.make_async_copy(error_hbm.at[:, cols], ge.at[pl.ds(ROWS, ROWS), cols], in_sem.at[1, i]),
            pltpu.make_async_copy(basis_hbm.at[:, cols], bt.at[:, cols], in_sem.at[2, i]),
        ]
        for copy in group:
            copy.start()
        loads.append(group)

    barrier = pltpu.get_barrier_semaphore()
    replicas = [(2, 1), (1, 1), (3, 1), (2, 0), (1, 0), (3, 0), (0, 1)]
    replicas = [at((y + dy) % NY, (c + dc) % 2, x, z) for dy, dc in replicas]
    plane = [(dx, dy) for dx in (2, 1, 3, 0) for dy in (2, 1, 3, 0)]
    others = replicas + [across(dx, dy) for dx, dy in plane if dx] + [along_z(d) for d in range(1, NZ)]
    for other in others:
        pl.semaphore_signal(barrier, inc=1, device_id=other, device_id_type=MESH)

    health = jnp.full((8, 128), 1.0 - overflow[0].astype(F32), F32)
    hb[0] = health
    weight = health[:1, :1]

    def corrected(start):
        cols = pl.ds(pl.multiple_of(start, 512), 512)
        return (ge[:ROWS, cols].astype(F32) + ge[ROWS:, cols].astype(F32)) * weight

    def project(start):
        cols = pl.ds(pl.multiple_of(start, 512), 1024)
        basis = jnp.concatenate(pieces(bt[:, cols]), axis=0)
        return lax.dot_general(basis, ge[:, cols], (((1,), (1,)), ((), ())), preferred_element_type=F32)

    for copy in loads[0]:
        copy.wait()
    acc = jnp.zeros((3 * RANK, 2 * ROWS), F32)
    for k in range(HALF // 1024):
        acc += project(halves[0] + k * 1024)
        for i in range(2):
            mo[:, pl.ds(k * 1024 + i * 512, 512)] = corrected(halves[0] + k * 1024 + i * 512)
    pl.semaphore_wait(barrier, len(others))
    send(hb.at[0], hb.at[1], 0, m_r.at[MPARTS], partner)
    for k in range(MPARTS):
        rows = pl.ds(k * (ROWS // MPARTS), ROWS // MPARTS)
        send(mo.at[rows], mi.at[rows], 1, m_r.at[k], partner)
    for copy in loads[1]:
        copy.wait()
    for k in range(HALF // 1024):
        acc += project(halves[1] + k * 1024)
    both = acc[:RANK] + acc[RANK : 2 * RANK] + acc[2 * RANK :]

    ly[rep] = (both[:, :ROWS] + both[:, ROWS:]) * weight
    for other in replicas:
        send(ly.at[rep], ly.at[rep], 2, ly_r.at[0], other)

    for k in range(MPARTS):
        size = ROWS // MPARTS
        rows = pl.ds(k * size, size)
        arrived(mi.at[rows], m_r.at[k])
        for i in range(HALF // 1024):
            own = pl.ds(pl.multiple_of(halves[1] + i * 1024, 1024), 1024)
            cols = pl.ds(i * 1024, 1024)
            value = ge[rows, own].astype(F32) + ge[pl.ds(ROWS + k * size, size), own].astype(F32)
            value = value * weight + mi[rows, cols]
            high = value.astype(BF16)
            mc[rows, cols] = high
            mc[pl.ds(ROWS + k * size, size), cols] = (value - high.astype(F32)).astype(BF16)
    arrived(hb.at[1], m_r.at[MPARTS])
    hs[y] = hb[0] + hb[1]
    for d in (2, 1, 3):
        send(hs.at[y], hs.at[y], 6, hs_r.at[0], across(0, d))

    arrived(ly.at[pl.ds(0, 7)], ly_r.at[0])
    left = ly[0]
    for i in range(1, 8):
        left = left + ly[i]

    gram = full_dot(left, jnp.concatenate([left] * 4, axis=0), ((1,), (1,)))
    lane_group = lax.broadcasted_iota(jnp.int32, (8, 128), 1) // RANK
    packed = gram[:8]
    for b in range(1, 4):
        packed = jnp.where(lane_group == b, gram[8 * b : 8 * b + 8], packed)
    gx[x] = packed
    for d in (2, 1, 3):
        send(gx.at[x], gx.at[x], 4, gx_r.at[0], across(d, 0))
    weighted = jnp.concatenate(pieces(left), axis=0)
    weighted = jnp.concatenate([weighted, weighted], axis=1)
    first = (x, y)
    second = (y, x)
    for d in (2, 1, 3, 0):
        for h in range(2):
            p = (first[h] + d) % 4
            group = [h * 16 + (p * 4 + q, q * 4 + p)[h] for q in range(4)]
            if h:
                rows = jnp.concatenate([mc[:, pl.ds(pl.multiple_of(b * 128, 128), 128)] for b in group], axis=1)
            else:
                rows = mc[:, pl.ds(pl.multiple_of(group[0] * 128, 512), 512)]
            out = lax.dot_general(weighted, rows, (((1,), (0,)), ((), ())), preferred_element_type=F32)
            value = out[:RANK] + out[RANK : 2 * RANK] + out[2 * RANK :]
            for q in range(4):
                part = value[:, q * 128 : (q + 1) * 128]
                if d == 0:
                    r1[h, p, q] = part
                else:
                    t1[h * 16 + p * 4 + q] = part
            if d:
                target = across(0, d) if h else across(d, 0)
                send(t1.at[pl.ds(h * 16 + p * 4, 4)], r1.at[h, first[h]], 3, p1_r.at[h], target)

    arrived(gx.at[pl.ds(0, 3)], gx_r.at[0])
    gz[z] = gx[0] + gx[1] + gx[2] + gx[3]
    for d in (4, 3, 5, 2, 6, 1, 7):
        send(gz.at[z], gz.at[z], 5, gz_r.at[0], along_z(d))

    for h in range(2):
        arrived(blocks(12), p1_r.at[h])
        for q in range(4):
            t2[h * 4 + q] = r1[h, 0, q] + r1[h, 1, q] + r1[h, 2, q] + r1[h, 3, q]
        for d in (2, 1, 3):
            q = (second[h] + d) % 4
            target = across(d, 0) if h else across(0, d)
            send(t2.at[h * 4 + q], r2.at[h * 4 + second[h]], 10, p2_r.at[h], target)
        r2[h * 4 + second[h]] = t2[h * 4 + second[h]]
    for h in range(2):
        arrived(blocks(3), p2_r.at[h])
        zb[h, z] = r2[h * 4] + r2[h * 4 + 1] + r2[h * 4 + 2] + r2[h * 4 + 3]
        for d in (4, 3, 5, 2, 6, 1, 7):
            send(zb.at[h, z], zb.at[h, z], 7, z_r.at[h], along_z(d))
    arrived(hs.at[pl.ds(0, 3)], hs_r.at[0])
    kept = hs[0] + hs[1] + hs[2] + hs[3]

    arrived(gz.at[pl.ds(0, 7)], gz_r.at[0])
    packed = gz[0]
    for i in range(1, NZ):
        packed = packed + gz[i]
    gram = jnp.concatenate([packed] + [pltpu.roll(packed, 128 - RANK * b, 1) for b in range(1, 4)], axis=0)
    inverse = inverse_factor(gram)[:, :RANK]

    me = slot(0, 0)
    for h in range(2):
        arrived(blocks(7), z_r.at[h])
        value = zb[h, 0]
        for i in range(1, NZ):
            value = value + zb[h, i]
        nb[c, h, me] = full_dot(inverse, value, ((1,), (0,))) / kept[:1]
        mine = nb.at[c, h, me]
        for dx, dy in plane[:-1]:
            send(mine, mine, 8, a_r.at[h, me], across(dx, dy))
        send(mine, mine, 9, ac_r.at[h], partner)
    ortho[...] = full_dot(inverse, left, ((1,), (0,)))
    all_sent(hb.at[0], 0)
    all_sent(mo, 1)
    all_sent(blocks(7), 2)
    all_sent(blocks(24), 3)
    all_sent(blocks(6), 10)
    all_sent(gx.at[pl.ds(0, 3)], 4)
    all_sent(gz.at[pl.ds(0, 7)], 5)
    all_sent(hs.at[pl.ds(0, 3)], 6)
    all_sent(blocks(14), 7)
    left_pieces = stacked(ortho[...])

    def finish(core, h):
        for k in range(QUARTER // WIDTH):
            cols = pl.ds(pl.multiple_of(core * HALF + h * QUARTER + k * WIDTH, WIDTH), WIDTH)
            values = [nb[core, h, k * (WIDTH // 128) + i] for i in range(WIDTH // 128)]
            apply(health[:1, :1], left_pieces, values, ge, update, new_error, new_basis, cols, cols)

    for h in range(2):
        for dx, dy in WAITS:
            source = slot(dx, dy)
            theirs = nb.at[c, h, source]
            arrived(theirs, a_r.at[h, source])
            send(theirs, theirs, 9, ac_r.at[h], partner)
        finish(c, h)
    arrived(blocks(16), ac_r.at[0])
    finish(1 - c, 0)
    arrived(blocks(16), ac_r.at[1])
    all_sent(blocks(30), 8)
    all_sent(blocks(32), 9)


def stacked(ortho):
    o1, o2, _ = pieces(ortho)
    return jnp.concatenate([o1, o1, o2], axis=0)


def apply(health, ortho_pieces, blocks, ge, update, new_error, basis, cols, to):
    value = jnp.concatenate(blocks, axis=1)
    basis[:, to] = value
    n1, n2, _ = pieces(value)
    approx = lax.dot_general(
        ortho_pieces, jnp.concatenate([n1, n2, n1], axis=0), (((0,), (0,)), ((), ())), preferred_element_type=F32
    )
    update[:, to] = approx.astype(BF16)
    error_value = ge[ROWS:, cols].astype(F32)
    corrected = ge[:ROWS, cols].astype(F32) + error_value
    new_error[:, to] = jnp.where(health > 0.5, corrected - approx, error_value).astype(BF16)


def last_kernel(
    overflow, nb, ortho, ge, update, new_error, basis, update_hbm, error_hbm, basis_hbm, update_s, error_s, basis_s, sem
):
    c = lax.axis_index("rep") % 2
    results = ((update, update_s, update_hbm), (new_error, error_s, error_hbm), (basis, basis_s, basis_hbm))
    copies = []
    for k, start in enumerate((c * HALF, c * HALF + QUARTER, (1 - c) * HALF)):
        cols = pl.ds(pl.multiple_of(start, QUARTER), QUARTER)
        for i, (done, _, out) in enumerate(results):
            copies.append(pltpu.make_async_copy(done.at[:, cols], out.at[:, cols], sem.at[i, k]))
            copies[-1].start()
    health = 1.0 - overflow[0].astype(F32)
    ortho_pieces = stacked(ortho[...])
    for k in range(QUARTER // WIDTH):
        to = pl.ds(k * WIDTH, WIDTH)
        cols = pl.ds(pl.multiple_of((1 - c) * HALF + QUARTER + k * WIDTH, WIDTH), WIDTH)
        values = [nb[1 - c, 1, k * (WIDTH // 128) + i] for i in range(WIDTH // 128)]
        apply(health, ortho_pieces, values, ge, update_s, error_s, basis_s, cols, to)
        for i, (_, new, out) in enumerate(results):
            copies.append(pltpu.make_async_copy(new.at[:, to], out.at[:, cols], sem.at[i, 3 + k]))
            copies[-1].start()
    for copy in copies:
        copy.wait()


def on_device(grad_out, error_out, basis_out, overflow):
    grad, error = grad_out[0], error_out[0]
    hbm = pl.BlockSpec(memory_space=pltpu.MemorySpace.HBM)
    smem, whole = pl.BlockSpec(memory_space=pltpu.SMEM), pl.BlockSpec(memory_space=pltpu.VMEM)
    dma = pltpu.SemaphoreType.DMA
    vmem = lambda *shape: pltpu.VMEM(shape, F32)
    block = (RANK, 128)
    operands = [pltpu.with_memory_space_constraint(a, pltpu.HBM) for a in (grad, error, basis_out.T)]
    outs = pl.pallas_call(
        reduce_kernel,
        out_shape=[
            vmem(2, 2, 16, *block),
            vmem(RANK, ROWS),
            pltpu.VMEM((2 * ROWS, D), BF16),
            pltpu.VMEM((ROWS, D), BF16),
            pltpu.VMEM((ROWS, D), BF16),
            vmem(RANK, D),
        ],
        in_specs=[hbm, hbm, hbm, smem],
        out_specs=[whole] * 6,
        scratch_shapes=[
            vmem(RANK, D),
            vmem(2, 8, 128),
            vmem(NY, 8, 128),
            vmem(ROWS, HALF),
            vmem(ROWS, HALF),
            pltpu.VMEM((2 * ROWS, HALF), BF16),
            vmem(8, *block),
            vmem(NX, 8, 128),
            vmem(NZ, 8, 128),
            vmem(32, *block),
            vmem(2, 4, 4, *block),
            vmem(8, *block),
            vmem(8, *block),
            vmem(2, NZ, *block),
            dma((3, 2)),
            dma((MPARTS + 1,)),
            dma((1,)),
            dma((1,)),
            dma((1,)),
            dma((1,)),
            dma((2,)),
            dma((2,)),
            dma((2,)),
            dma((2, 16)),
            dma((2,)),
            dma((11,)),
        ],
        compiler_params=pltpu.CompilerParams(collective_id=0, has_side_effects=True, vmem_limit_bytes=32 << 20),
        name="reduce",
    )(*operands, overflow)

    update, new_error, new_basis = pl.pallas_call(
        last_kernel,
        out_shape=[
            jax.ShapeDtypeStruct((ROWS, D), BF16),
            jax.ShapeDtypeStruct((ROWS, D), BF16),
            jax.ShapeDtypeStruct((RANK, D), F32),
        ],
        in_specs=[smem] + [whole] * 6,
        out_specs=[hbm, hbm, hbm],
        scratch_shapes=[
            pltpu.VMEM((ROWS, QUARTER), BF16), pltpu.VMEM((ROWS, QUARTER), BF16), vmem(RANK, QUARTER), dma((3, 3 + QUARTER // WIDTH))
        ],
        compiler_params=pltpu.CompilerParams(vmem_limit_bytes=16 << 20),
        name="last",
    )(overflow, *outs)
    return update, new_error[None], new_basis.T


def solution(mesh):
    return jax.shard_map(
        on_device,
        mesh=mesh,
        in_specs=(P("rep", "shard", None), P("rep", "shard", None), P(), P("rep")),
        out_specs=(P("shard", None), P("rep", "shard", None), P()),
        check_vma=False,
    )
```
